768 devices in a mesh: box: 64 (over x, y, core), grp: 12 (over z).
Axes of the slice: x: 4, y: 8, z: 12, core: 2. Of those that a mesh axis runs over, the one named last changes fastest.
Arguments:
- source: bfloat16 [122880, 32, 32], P(('box', 'grp')), may hold values from -6 to 6
- conductivity: bfloat16 [122880, 32, 32], P(('box', 'grp')), may hold values from 0.25 to 4
- new_owner: int32 [64, 12, 5, 1], P('box', 'grp'), may hold values from 0 to 11; in each aligned block of 5 rows (0 to 4, 5 to 9, ..., all dimensions but the last counted through in order) at most 2 rows name the same one
Outputs:
- correction: bfloat16 [64, 12, 12, 2, 32768], P('box', 'grp')
- coarse_residual: float32 [12, 320, 4096], P('grp')
The draws below stay inside these ranges and needn't reach their ends.
Inputs may be any that keep to these rules, and one draw needn't show every extreme that they name: `new_owner`: boxes move only within their box index; among the 5 boxes of one device at most 2 share a new owner, and in every draw some device gives exactly 2 boxes to one owner.
All inputs are finite; a program needn't handle non-finite values.
Results may differ from the reference program's by a relative error of at most 0.001.
Values may be sent and summed in bfloat16 or wider, within the bound.
No kernel may reach another device: no remote copies, remote signals or barrier semaphores. Data moves between devices by JAX's collectives and lax.ppermute only.
A program may use at most 128 MiB of HBM per device.

```python
import math
import jax
import jax.numpy as jnp
import numpy as np
from jax import lax

BZ = 32
BY = 32
BX = 32
B_DEV = 5
CAP = 2
NZ = 122880
CELLS = 32768
RC = 4096
N_BOX = 64
N_GRP = 12
DEVICES = 768


def block_levels(rng, shape, shards, least, high):
    level = 1.0
    for dim, parts in shards:
        steps = jax.random.uniform(jax.random.fold_in(jax.random.fold_in(rng, 6), dim), (parts,), jnp.float32, least / len(shards), high / len(shards))
        level = level * jnp.repeat(jnp.exp(steps), shape[dim] // parts).reshape((-1,) + (1,) * (len(shape) - 1 - dim))
    return level


def routed_block(stream_key, own, number, rows, number_of, top, most, skew):
    ranking = jax.random.permutation(stream_key, number_of)
    packed, common = load_shares(number_of, rows * top, most, skew, True), load_shares(number_of, rows * top, most, skew, False)
    places = jnp.arange(number_of)

    def named(sizes, rotation):
        used = int((sizes > 0).sum())
        fixed = max(1, used // 4)
        passed = fixed + (places - fixed + rotation * (used - fixed)) % max(1, number_of - fixed)
        return jnp.zeros((number_of,), jnp.int32).at[ranking[jnp.where(places < fixed, places, passed)]].set(jnp.asarray(sizes, jnp.int32))

    sizes = jnp.where(number % 4 == 0, named(packed, number // 4), named(common, number - number // 4 - 1))
    mixed = jax.random.permutation(jax.random.fold_in(own, 3), number_of)
    donor, sink = mixed[0:number_of // 2 * 2:2], mixed[1:number_of // 2 * 2:2]
    room = jnp.minimum(sizes[donor] - 1, most - sizes[sink]) // 2
    room = jnp.where((donor == ranking[0]) | (sink == ranking[0]) | (sizes[sink] == 0), 0, jnp.maximum(room, 0))
    passed = jax.random.randint(jax.random.fold_in(own, 4), (number_of // 2,), 0, 1 << 20) % (room + 1)
    sizes = sizes.at[donor].add(-passed).at[sink].add(passed)
    items = jnp.searchsorted(jnp.cumsum(sizes), jnp.arange(rows * top), side="right").astype(jnp.int32)
    grid = items.reshape(top, rows).T
    grid = grid[jax.random.permutation(jax.random.fold_in(own, 1), rows)]
    rotation = jax.random.randint(jax.random.fold_in(own, 2), (rows, 1), 0, top)
    return jnp.take_along_axis(grid, (jnp.arange(top)[None, :] + rotation) % top, axis=1)


def load_shares(count, total, reach, lean, full):
    portions = [(1 << 20) // math.isqrt(grade ** lean) + 1 for grade in range(1, count + 1)]
    largest = reach if full else min(reach, max(-(-total // count), total * portions[0] // sum(portions)))
    least = 1 if total - largest >= count - 1 else 0
    counts, spare = [largest] + [least] * (count - 1), total - largest - least * (count - 1)
    while spare > 0:
        free = [i for i in range(1, count) if counts[i] < largest] or [i for i in range(1, count) if counts[i] < reach]
        pool, left = sum([portions[i] for i in free]), spare
        for i in free:
            addition = min(reach - counts[i], max(1, left * portions[i] // pool), spare)
            counts[i] = counts[i] + addition
            spare = spare - addition
    return np.array(counts)


def scatter_about(rng, dims, deviation, reach, shards=(), kind=jnp.bfloat16):
    loudness = block_levels(rng, dims, shards, -0.22, 0.18) if shards else 1.0
    array = jax.random.normal(rng, dims, jnp.float32) * deviation * loudness
    return jnp.minimum(jnp.maximum(array, -reach), reach).astype(kind)


def setup_inputs(seed: int = 0) -> dict:
    key_list = jax.random.split(jax.random.key(seed), 4)
    source = scatter_about(key_list[0], (NZ, BY, BX), 1.0, 6.0, ((0, 768),))
    conductivity = jnp.clip(jnp.exp(math.log(4.0) - 2.7725887 * jax.random.uniform(key_list[1], (NZ, BY, BX), jnp.float32) ** block_levels(key_list[1], (NZ, BY, BX), ((0, 768),), -0.2, 0.2)), 0.25, 4.0).astype(jnp.bfloat16)
    new_owner_keys = jax.random.split(jax.random.fold_in(key_list[2], 1), N_BOX * N_GRP * B_DEV // B_DEV)
    new_owner_turns = jax.random.permutation(jax.random.fold_in(key_list[2], 3), N_BOX * N_GRP * B_DEV // B_DEV)
    new_owner = jax.vmap(lambda own, number: routed_block(jax.random.fold_in(key_list[2], 2), own, number, B_DEV, N_GRP, 1, CAP, 2))(new_owner_keys, new_owner_turns).reshape((N_BOX, N_GRP, B_DEV, 1))
    return dict(source=source, conductivity=conductivity, new_owner=new_owner)


WEIGHT = 0.8


def shift_next(values_in, which):
    extent = values_in.shape[which]
    widths = [(0, 0)] * values_in.ndim
    widths[which] = (0, 1)
    return jnp.pad(lax.slice_in_dim(values_in, 1, extent, axis=which), widths)


def shift_prev(values_in, which):
    extent = values_in.shape[which]
    widths = [(0, 0)] * values_in.ndim
    widths[which] = (1, 0)
    return jnp.pad(lax.slice_in_dim(values_in, 0, extent - 1, axis=which), widths)


def smooth(source, conductivity):
    inside = conductivity > 0
    axes_list = (conductivity.ndim - 3, conductivity.ndim - 2, conductivity.ndim - 1)
    face_list = []
    diagonal = jnp.zeros_like(conductivity)
    for which in axes_list:
        after = shift_next(conductivity, which)
        face_fwd = jnp.where(inside & (after > 0), 0.5 * (conductivity + after), 0.0)
        face_list.append(face_fwd)
        before = shift_prev(conductivity, which)
        face_bwd = shift_prev(face_fwd, which)
        diagonal = diagonal + jnp.where(after > 0, face_fwd, conductivity)
        diagonal = diagonal + jnp.where(before > 0, face_bwd, conductivity)
    divisor = jnp.where(inside, diagonal, 1.0)

    def operate(values_in):
        result = diagonal * values_in
        for which, face_fwd in zip(axes_list, face_list):
            result = result - face_fwd * shift_next(values_in, which)
            result = result - shift_prev(face_fwd * values_in, which)
        return result

    sweep_one = jnp.where(inside, WEIGHT * source / divisor, 0.0)
    sweep_two = jnp.where(inside, sweep_one + WEIGHT * (source - operate(sweep_one)) / divisor, 0.0)
    leftover = jnp.where(inside, source - operate(sweep_two), 0.0)
    return sweep_two, leftover


def restrict(leftover):
    leading = leftover.shape[:-3]
    layers, rows_y, rows_x = leftover.shape[-3:]
    blocks = leftover.reshape(leading + (layers // 2, 2, rows_y // 2, 2, rows_x // 2, 2))
    return jnp.mean(blocks, axis=(-5, -3, -1)).reshape(leading + (-1,))


def reference(source, conductivity, new_owner):
    layers_dev = B_DEV * BZ
    padded = jnp.pad(jnp.stack([source, conductivity]), ((0, 0), (3, 3), (0, 0), (0, 0)))

    def per_device(index):
        start = (index * layers_dev).astype(jnp.int32)
        block = lax.dynamic_slice_in_dim(padded, start, layers_dev + 6, axis=1).astype(jnp.float32)
        sweep_two, leftover = smooth(block[0], block[1])
        settled_box = sweep_two[3:3 + layers_dev].reshape(B_DEV, CELLS).astype(jnp.bfloat16)
        coarse_box = restrict(leftover[3:3 + layers_dev].reshape(B_DEV, BZ, BY, BX))
        return settled_box, coarse_box

    settled, coarse_all = lax.map(per_device, jnp.arange(DEVICES, dtype=jnp.int32))
    coarse = coarse_all.reshape(N_BOX, N_GRP, B_DEV, RC).transpose(1, 0, 2, 3).reshape(N_GRP, N_BOX * B_DEV, RC)
    settled = settled.reshape(N_BOX, N_GRP, B_DEV, CELLS)
    owners = new_owner.reshape(N_BOX, N_GRP, B_DEV)
    order = jnp.arange(B_DEV)
    earlier = (owners[..., :, None] == owners[..., None, :]) & (order[:, None] < order[None, :])
    rank_in = jnp.sum(earlier.astype(jnp.int32), axis=-2).astype(jnp.int32)
    senders = jnp.broadcast_to(jnp.arange(N_BOX, dtype=jnp.int32)[:, None, None], owners.shape)
    groups = jnp.broadcast_to(jnp.arange(N_GRP, dtype=jnp.int32)[None, :, None], owners.shape)
    correction = jnp.zeros((N_BOX, N_GRP, N_GRP, CAP, CELLS), jnp.bfloat16)
    correction = correction.at[senders, owners, groups, rank_in].set(settled)
    return correction, coarse
```

```python
import functools

import jax
import jax.numpy as jnp
from jax import lax
from jax.experimental import pallas as pl
from jax.experimental.pallas import tpu as pltpu
from jax.sharding import Mesh, PartitionSpec as P

WEIGHT = 0.8
F32, BF16, F16 = jnp.float32, jnp.bfloat16, jnp.float16
HALO = 3
EDGE = 4
SUB, LANES = 8, 128
VMEM_LIMIT = 40 * 1024 * 1024


def _iota(shape, dim):
    return lax.broadcasted_iota(jnp.int32, shape, dim)


def _chunks(lo, hi, step, body):
    whole = (hi - lo) // step
    if whole:

        @pl.loop(0, whole)
        def _(i):
            body(lo + i * step, step)

    if lo + whole * step < hi:
        body(lo + whole * step, hi - lo - whole * step)


def _load(ref, layer, count):
    if isinstance(layer, int):
        rows = ref[layer * SUB : (layer + count) * SUB, :]
    else:
        rows = ref[pl.ds(pl.multiple_of(layer * SUB, SUB), count * SUB), :]
    return rows.reshape(count, SUB, LANES)


def _store(ref, layer, value):
    count = value.shape[0]
    rows = value.reshape(count * SUB, LANES)
    if isinstance(layer, int):
        ref[layer * SUB : (layer + count) * SUB, :] = rows
    else:
        ref[pl.ds(pl.multiple_of(layer * SUB, SUB), count * SUB), :] = rows


def _next_x(v):
    return pltpu.roll(v, LANES - 1, 2)


def _prev_x(v):
    return pltpu.roll(v, 1, 2)


def _next_y(v):
    turned = pltpu.roll(v, LANES - 32, 2)
    return jnp.where(_iota(v.shape, 2) < 96, turned, pltpu.roll(turned, SUB - 1, 1))


def _prev_y(v):
    turned = pltpu.roll(v, 32, 2)
    return jnp.where(_iota(v.shape, 2) >= 32, turned, pltpu.roll(turned, 1, 1))


def _transposed(cells_ref, out_ref, layer_of, layers):
    total = cells_ref.shape[1]
    pick = (_iota((layers, total), 1) == layer_of(_iota((layers, total), 0))).astype(BF16)
    for j in range(SUB):
        part = lax.dot_general(
            pick,
            cells_ref[j * LANES : (j + 1) * LANES, :],
            (((1,), (1,)), ((), ())),
            preferred_element_type=F32,
        )
        out_ref[pl.ds(j, layers, stride=SUB), :] = part


def _sweeps(c_ref, f_ref, gx_ref, gy_ref, gz_ref, w_ref, u1_ref, u2_ref, t_ref, lo, hi, ends):
    lo, hi = lo - 2, hi + 2

    def faces(layer, count):
        shape = (count, SUB, LANES)
        sub, lane = _iota(shape, 1), _iota(shape, 2)
        x, y = lane % 32, sub * 4 + lane // 32
        c = _load(c_ref, layer, count)
        after, before = _load(c_ref, layer + 1, count), _load(c_ref, layer - 1, count)
        gx = jnp.where(x < 31, 0.5 * (c + _next_x(c)), 0.0)
        gy = jnp.where(y < 31, 0.5 * (c + _next_y(c)), 0.0)
        gz, gz_before = 0.5 * (c + after), 0.5 * (c + before)
        outer = (x == 0).astype(F32) + (x == 31).astype(F32) + (y == 0).astype(F32) + (y == 31).astype(F32)
        diagonal = gx + _prev_x(gx) + gy + _prev_y(gy) + c * outer
        if ends:
            diagonal = diagonal + jnp.where(after > 0, gz, c) + jnp.where(before > 0, gz_before, c)
            diagonal = jnp.where(c > 0, diagonal, 1.0)
            gz = jnp.where((c > 0) & (after > 0), gz, 0.0)
        else:
            diagonal = diagonal + gz + gz_before
        weight = WEIGHT / diagonal
        _store(gx_ref, layer, gx)
        _store(gy_ref, layer, gy)
        _store(gz_ref, layer, gz)
        _store(w_ref, layer, weight)
        _store(u1_ref, layer, weight * _load(f_ref, layer, count))

    _chunks(lo, hi, 5, faces)
    lo, hi = lo + 1, hi - 1

    def second(layer, count):
        pulled = _pull(u1_ref, gx_ref, gy_ref, gz_ref, layer, count)
        f = _load(f_ref, layer, count)
        _store(u2_ref, layer, _load(w_ref, layer, count) * ((2.0 - WEIGHT) * f + pulled))
        _store(t_ref, layer, (1.0 - WEIGHT) ** 2 * f - WEIGHT * pulled)

    _chunks(lo, hi, 7, second)


def _pull(u_ref, gx_ref, gy_ref, gz_ref, layer, count):
    u = _load(u_ref, layer, count)
    gx, gy = _load(gx_ref, layer, count), _load(gy_ref, layer, count)
    total = gx * _next_x(u) + _prev_x(gx * u)
    total = total + gy * _next_y(u) + _prev_y(gy * u)
    total = total + _load(gz_ref, layer, count) * _load(u_ref, layer + 1, count)
    return total + _load(gz_ref, layer - 1, count) * _load(u_ref, layer - 1, count)


def _residual(u2_ref, t_ref, gx_ref, gy_ref, gz_ref, pair_ref, out_ref, lo, hi, pair_at, out_at):
    def body(layer, count):
        left = _load(t_ref, layer, count) + _pull(u2_ref, gx_ref, gy_ref, gz_ref, layer, count)
        pairs = left.reshape(count // 2, 2, SUB, LANES)
        _store(pair_ref, (layer - lo) // 2 + pair_at, pairs[:, 0] + pairs[:, 1])
        rows = _load(u2_ref, layer, count).reshape(count * SUB, LANES).astype(BF16)
        out_ref[pl.ds(pl.multiple_of((layer - lo + out_at) * SUB, 16), count * SUB), :] = rows

    _chunks(lo, hi, 8, body)


def _pooled(pair_ref, rows):
    lane, to = _iota((LANES, LANES), 0), _iota((LANES, LANES), 1)
    place = (lane // 64) * 16 + (lane % 32) // 2
    total = jnp.zeros((rows, LANES), F32)
    for k in range(4):
        part = pair_ref[pl.ds(k, rows, stride=4), :]
        pick = jnp.where(to == place + 32 * k, 0.125, 0.0).astype(BF16)
        high = part.astype(BF16)
        rest = part - high.astype(F32)
        low = rest.astype(BF16)
        lowest = (rest - low.astype(F32)).astype(BF16)
        for term in (high, low, lowest):
            total = total + jnp.dot(term, pick, preferred_element_type=F32)
    return total


def edges_kernel(layers, f_in, c_in, first_ref, last_ref, f_ref, c_ref):
    def layer_of(row):
        return jnp.where(row < HALO, row, jnp.where(row < 2 * HALO, row + layers - 2 * HALO, -1))

    rows = HALO * SUB
    for at, (cells, ref) in enumerate(((f_in, f_ref), (c_in, c_ref))):
        _transposed(cells, ref, layer_of, 8)
        edges = ref[: 2 * rows, :].astype(BF16)
        first_ref[at * rows : (at + 1) * rows, :] = edges[:rows]
        last_ref[at * rows : (at + 1) * rows, :] = edges[rows:]


def inner_kernel(layers, boxes, owner_ref, f_in, c_in, near_ref, sent_ref, coarse_ref, c_ref, f_ref, *work):
    for cells, ref in ((f_in, f_ref), (c_in, c_ref)):
        _transposed(cells, ref, lambda row: row, layers)
    rows = (EDGE + HALO) * SUB
    for at, ref in enumerate((f_ref, c_ref)):
        near_ref[2 * at * rows : (2 * at + 1) * rows, :] = ref[:rows, :].astype(BF16)
        near_ref[(2 * at + 1) * rows : (2 * at + 2) * rows, :] = ref[layers * SUB - rows :, :].astype(BF16)
    gx, gy, gz, w, u1, u2, t, pair = work
    _sweeps(c_ref, f_ref, gx, gy, gz, w, u1, u2, t, EDGE - 1, layers - EDGE + 1, False)
    blank = EDGE // 2 * SUB
    pair[:blank, :] = jnp.zeros((blank, LANES), F32)
    pair[layers // 2 * SUB - blank :, :] = jnp.zeros((blank, LANES), F32)
    _residual(u2, t, gx, gy, gz, pair, sent_ref, EDGE, layers - EDGE, EDGE // 2, EDGE)
    coarse_ref[...] = _pooled(pair, coarse_ref.shape[0])
    sent_ref[: EDGE * SUB, :] = jnp.zeros((EDGE * SUB, LANES), BF16)
    sent_ref[(layers - EDGE) * SUB : layers * SUB, :] = jnp.zeros((EDGE * SUB, LANES), BF16)
    named = _iota((16, LANES), 0)
    owners = jnp.zeros((16, LANES), F32)
    for k in range(boxes):
        owners = jnp.where(named == k, owner_ref[k].astype(F32), owners)
    sent_ref[layers * SUB :, :] = owners.astype(BF16)


def outer_kernel(layers, before_ref, after_ref, near_ref, inner_ref, sent_in, coarse_ref, sent_ref, c_ref, f_ref, gx, gy, gz, w, u1, u2, t, pair, out_ref, sems):
    del sent_in
    span = EDGE + 2 * HALO
    total = 2 * span
    halo, own = HALO * SUB, (EDGE + HALO) * SUB
    for at, ref in enumerate((f_ref, c_ref)):
        ref[:halo, :] = before_ref[at * halo : (at + 1) * halo, :].astype(F32)
        ref[halo : span * SUB, :] = near_ref[2 * at * own : (2 * at + 1) * own, :].astype(F32)
        ref[span * SUB : total * SUB - halo, :] = near_ref[(2 * at + 1) * own : (2 * at + 2) * own, :].astype(F32)
        ref[total * SUB - halo :, :] = after_ref[at * halo : (at + 1) * halo, :].astype(F32)
    _sweeps(c_ref, f_ref, gx, gy, gz, w, u1, u2, t, HALO, total - HALO, True)
    for at in range(2):
        lo = HALO + at * span
        _residual(u2, t, gx, gy, gz, pair, out_ref, lo, lo + EDGE, at * EDGE // 2, at * EDGE)
    copies = []
    for at, row in enumerate((0, (layers - EDGE) * SUB)):
        copies.append(
            pltpu.make_async_copy(
                out_ref.at[pl.ds(at * EDGE * SUB, EDGE * SUB), :],
                sent_ref.at[pl.ds(row, EDGE * SUB), :],
                sems.at[at],
            )
        )
        copies[-1].start()
    outer = _pooled(pair, SUB)
    inner = inner_ref[...]
    peak = jnp.maximum(jnp.max(jnp.abs(outer)), jnp.max(jnp.abs(inner)))
    power = jnp.floor(jnp.log2(jnp.clip(jnp.full((16, LANES), peak, F32), 1e-30, 1e30)))
    scale = jnp.exp2(-power)[:1, :]
    rows = inner.shape[0]
    low = _iota((SUB, LANES), 0) < EDGE
    coarse_ref[:SUB, :] = jnp.where(low, outer, inner[:SUB]) * scale
    coarse_ref[SUB : rows - SUB, :] = inner[SUB : rows - SUB] * scale
    coarse_ref[rows - SUB : rows, :] = jnp.where(low, inner[rows - SUB :], outer) * scale
    coarse_ref[rows:, :] = power
    for copy in copies:
        copy.wait()


def select_kernel(senders, box_rows, boxes, all_ref, out_ref, named_ref, which_ref, table_ref, box_ref, mixed_ref, done_ref, small_sems, in_sems, out_sems):
    rows = boxes * box_rows
    copy = pltpu.make_async_copy(all_ref.at[:, pl.ds(rows, 16), :], named_ref, small_sems.at[0])
    copy.start()
    copy.wait()
    me = lax.axis_index("grp").astype(F32)
    named = named_ref[...].astype(F32)
    number = _iota(named.shape, 1)
    mine = (named == me) & (number < boxes)
    first = jnp.min(jnp.where(mine, number, boxes), axis=1)
    last = jnp.max(jnp.where(mine, number, -1), axis=1)
    which_ref[0:senders, :] = jnp.where(last >= 0, first, -1)
    which_ref[senders : 2 * senders, :] = jnp.where(last > first, last, -1)
    copy = pltpu.make_async_copy(which_ref, table_ref, small_sems.at[1])
    copy.start()
    copy.wait()

    def fetch(sender, rank):
        box = jnp.maximum(table_ref[rank * senders + sender, 0], 0)
        start = pl.multiple_of(box * box_rows, box_rows)
        return pltpu.make_async_copy(
            all_ref.at[sender, pl.ds(start, box_rows), :], box_ref.at[sender, rank], in_sems.at[sender, rank]
        )

    for sender in range(senders):
        for rank in range(2):
            fetch(sender, rank).start()
    for sender in range(senders):
        for rank in range(2):
            fetch(sender, rank).wait()
            there = (table_ref[rank * senders + sender, 0] >= 0).astype(F32)
            mixed_ref[sender % 2, pl.ds(rank, box_rows, stride=2), :] = jnp.where(there > 0, box_ref[sender, rank].astype(F32), 0.0)
        done_ref[sender] = mixed_ref[sender % 2].astype(BF16)
        pltpu.make_async_copy(done_ref.at[sender], out_ref.at[sender], out_sems.at[sender]).start()
    for sender in range(senders):
        pltpu.make_async_copy(done_ref.at[sender], out_ref.at[sender], out_sems.at[sender]).wait()


def spread_kernel(sizes, block_rows, box_rows, boxes, in_ref, out_ref, mixed_ref):
    step = pl.program_id(0)
    x_count, y_count, core_count = sizes
    row = 0
    for d in range(8):
        device = step * 8 + d
        core, y, x = device % core_count, device // core_count % y_count, device // core_count // y_count
        start = ((y * core_count + core) * x_count + x) * block_rows
        power = in_ref[pl.ds(pl.multiple_of(start + boxes * box_rows, 16), 16), :]
        scale = jnp.exp2(power)[:1, :]
        for k in range(boxes):
            part = in_ref[pl.ds(pl.multiple_of(start + k * box_rows, 16), box_rows), :]
            mixed_ref[row * box_rows : (row + 1) * box_rows, :] = part * scale
            row += 1
    for group in range(row // 8):
        for lane in range(box_rows):
            tile = mixed_ref[pl.ds(group * 8 * box_rows + lane, 8, stride=box_rows), :]
            out_ref[group * 8 : (group + 1) * 8, lane * LANES : (lane + 1) * LANES] = tile


def _params():
    return pltpu.CompilerParams(vmem_limit_bytes=VMEM_LIMIT)


def _whole(count):
    return [pl.BlockSpec(memory_space=pltpu.VMEM)] * count


def _scratch(layers, pair_layers):
    return [pltpu.VMEM((layers * SUB, LANES), F32)] * 9 + [pltpu.VMEM((pair_layers * SUB, LANES), F32)]


def shards(sizes, source, conductivity, new_owner):
    layers, rows_y, rows_x = source.shape
    boxes = new_owner.shape[2]
    depth = layers // boxes
    group_count = lax.axis_size("grp")
    box_rows = depth * SUB
    coarse_rows = depth * SUB * LANES // 8 // LANES
    inner_boxes = boxes - 2
    f_in = jnp.transpose(source, (1, 2, 0)).reshape(rows_y * rows_x, layers)
    c_in = jnp.transpose(conductivity, (1, 2, 0)).reshape(rows_y * rows_x, layers)
    owners = new_owner.reshape(boxes)

    edge = jax.ShapeDtypeStruct((2 * HALO * SUB, LANES), BF16)
    first, last = pl.pallas_call(
        functools.partial(edges_kernel, layers),
        out_shape=[edge, edge],
        in_specs=_whole(2),
        out_specs=_whole(2),
        scratch_shapes=[pltpu.VMEM((8 * SUB, LANES), F32)] * 2,
        compiler_params=_params(),
        cost_estimate=pl.CostEstimate(flops=10**7, bytes_accessed=10**6, transcendentals=0),
        name="edge_layers",
    )(f_in, c_in)
    everyone = ("x", "y", "core", "grp")
    count = lax.axis_size(everyone)
    before = lax.ppermute(last, everyone, [(i, i + 1) for i in range(count - 1)])
    after = lax.ppermute(first, everyone, [(i + 1, i) for i in range(count - 1)])

    sent_shape = jax.ShapeDtypeStruct((boxes * box_rows + 16, LANES), BF16)
    near, sent, coarse_inner = pl.pallas_call(
        functools.partial(inner_kernel, layers, boxes),
        out_shape=[
            jax.ShapeDtypeStruct((4 * (EDGE + HALO) * SUB, LANES), BF16),
            sent_shape,
            jax.ShapeDtypeStruct((boxes * coarse_rows, LANES), F32),
        ],
        in_specs=[pl.BlockSpec(memory_space=pltpu.SMEM)] + _whole(2),
        out_specs=_whole(3),
        scratch_shapes=_scratch(layers, layers // 2),
        compiler_params=_params(),
        cost_estimate=pl.CostEstimate(flops=10**8, bytes_accessed=10**7, transcendentals=0),
        name="inner_layers",
    )(owners, f_in, c_in)

    total = 2 * (EDGE + 2 * HALO)
    coarse, sent = pl.pallas_call(
        functools.partial(outer_kernel, layers),
        out_shape=[jax.ShapeDtypeStruct((boxes * coarse_rows + 16, LANES), F32), sent_shape],
        in_specs=_whole(4) + [pl.BlockSpec(memory_space=pl.ANY)],
        out_specs=_whole(1) + [pl.BlockSpec(memory_space=pl.ANY)],
        scratch_shapes=_scratch(total, EDGE)
        + [pltpu.VMEM((2 * EDGE * SUB, LANES), BF16), pltpu.SemaphoreType.DMA((2,))],
        input_output_aliases={4: 1},
        compiler_params=_params(),
        name="outer_layers",
    )(before, after, near, coarse_inner, sent)

    got = lax.all_gather(sent, "grp", axis=0, tiled=True)
    gathered = coarse.astype(F16)
    for axes in ("x", ("y", "core")):
        gathered = lax.all_gather(gathered, axes, axis=0, tiled=True)

    senders = group_count
    correction = pl.pallas_call(
        functools.partial(select_kernel, senders, box_rows, boxes),
        out_shape=jax.ShapeDtypeStruct((senders, 2 * box_rows, LANES), BF16),
        in_specs=[pl.BlockSpec(memory_space=pltpu.HBM)],
        out_specs=pl.BlockSpec(memory_space=pl.ANY),
        scratch_shapes=[
            pltpu.VMEM((senders, 16, LANES), BF16),
            pltpu.VMEM((2 * senders, LANES), jnp.int32),
            pltpu.SMEM((2 * senders, LANES), jnp.int32),
            pltpu.VMEM((senders, 2, box_rows, LANES), BF16),
            pltpu.VMEM((2, 2 * box_rows, LANES), F32),
            pltpu.VMEM((senders, 2 * box_rows, LANES), BF16),
            pltpu.SemaphoreType.DMA((2,)),
            pltpu.SemaphoreType.DMA((senders, 2)),
            pltpu.SemaphoreType.DMA((senders,)),
        ],
        compiler_params=_params(),
        name="select_boxes",
    )(got.reshape(senders, boxes * box_rows + 16, LANES))
    correction = correction.reshape(senders, box_rows, 2, LANES).transpose(0, 2, 1, 3)

    devices = sizes[0] * sizes[1] * sizes[2]
    coarse_all = pl.pallas_call(
        functools.partial(spread_kernel, sizes, coarse.shape[0], coarse_rows, boxes),
        out_shape=jax.ShapeDtypeStruct((devices * boxes, coarse_rows * LANES), F32),
        grid=(devices // 8,),
        in_specs=_whole(1),
        out_specs=pl.BlockSpec((8 * boxes, coarse_rows * LANES), lambda i: (i, 0)),
        scratch_shapes=[pltpu.VMEM((8 * boxes * coarse_rows, LANES), F32)],
        compiler_params=_params(),
        name="spread_coarse",
    )(gathered.astype(F32))
    return (
        correction.reshape(1, 1, senders, 2, box_rows * LANES),
        coarse_all[None],
    )


def solution(mesh):
    sizes = (4, 8, 2) if mesh.shape["box"] == 64 else (1, 8, 2)
    fine = Mesh(mesh.devices.reshape(sizes + (mesh.shape["grp"],)), ("x", "y", "core", "grp"))
    box = ("x", "y", "core")
    return jax.shard_map(
        functools.partial(shards, sizes),
        mesh=fine,
        in_specs=(
            P(box + ("grp",), None, None),
            P(box + ("grp",), None, None),
            P(box, "grp", None, None),
        ),
        out_specs=(P(box, "grp", None, None, None), P("grp", None, None)),
        check_vma=False,
    )
```

```python
import functools

import jax
import jax.numpy as jnp
from jax import lax
from jax.experimental import pallas as pl
from jax.experimental.pallas import tpu as pltpu
from jax.sharding import Mesh, PartitionSpec as P

WEIGHT = 0.8
F32, BF16, F16 = jnp.float32, jnp.bfloat16, jnp.float16
HALO = 3
STEP = 40
EDGE = 2
SIDE = 4
SUB, LANES = 8, 128
VMEM_LIMIT = 40 * 1024 * 1024


def _iota(shape, dim):
    return lax.broadcasted_iota(jnp.int32, shape, dim)


def _chunks(lo, hi, step, body):
    whole = (hi - lo) // step
    if whole:

        @pl.loop(0, whole)
        def _(i):
            body(lo + i * step, step)

    if lo + whole * step < hi:
        body(lo + whole * step, hi - lo - whole * step)


def _load(ref, layer, count, shift=0):
    if isinstance(layer, int):
        rows = ref[layer * SUB + shift : (layer + count) * SUB + shift, :]
    elif shift:
        rows = ref[pl.ds(layer * SUB + shift, count * SUB), :]
    else:
        rows = ref[pl.ds(pl.multiple_of(layer * SUB, SUB), count * SUB), :]
    return rows.reshape(count, SUB, LANES)


def _store(ref, layer, value):
    count = value.shape[0]
    rows = value.reshape(count * SUB, LANES)
    if isinstance(layer, int):
        ref[layer * SUB : (layer + count) * SUB, :] = rows
    else:
        ref[pl.ds(pl.multiple_of(layer * SUB, SUB), count * SUB), :] = rows


def _beside(ref, layer, count):
    here = _load(ref, layer, count)
    lane = _iota((1, SUB, LANES), 2)
    below = jnp.where(lane < 32, _load(ref, layer, count, 1), here)
    above = jnp.where(lane >= 96, _load(ref, layer, count, -1), here)
    return (
        pltpu.roll(here, LANES - 1, 2),
        pltpu.roll(here, 1, 2),
        pltpu.roll(below, LANES - 32, 2),
        pltpu.roll(above, 32, 2),
    )


def _transposed(cells_ref, out_ref, layer_of, layers, at=0):
    total = cells_ref.shape[1]
    pick = (_iota((layers, total), 1) == layer_of(_iota((layers, total), 0))).astype(BF16)
    for j in range(SUB):
        part = lax.dot_general(
            pick,
            cells_ref[j * LANES : (j + 1) * LANES, :],
            (((1,), (1,)), ((), ())),
            preferred_element_type=F32,
        )
        out_ref[pl.ds(at * SUB + j, layers, stride=SUB), :] = part


def _sweeps(c_ref, f_ref, g_refs, gz_ref, w_ref, u1_ref, u2_ref, t_ref, lo, hi, ends):
    lo, hi = lo - 2, hi + 2
    sub, lane = _iota((1, SUB, LANES), 1), _iota((1, SUB, LANES), 2)
    x, y = lane & 31, sub * 4 + (lane >> 5)
    sides = (x == 31, x == 0, y == 31, y == 0)
    halves = [jnp.where(side, 0.0, 0.5) for side in sides]
    outer = sum(side.astype(F32) for side in sides)

    def faces(layer, count):
        c = _load(c_ref, layer, count)
        after, before = _load(c_ref, layer + 1, count), _load(c_ref, layer - 1, count)
        gz, gz_before = 0.5 * (c + after), 0.5 * (c + before)
        diagonal = c * outer
        if ends:
            diagonal = diagonal + jnp.where(after > 0, gz, c) + jnp.where(before > 0, gz_before, c)
            gz = jnp.where((c > 0) & (after > 0), gz, 0.0)
        else:
            diagonal = diagonal + (gz + gz_before)
        _store(gz_ref, layer, gz)
        for half, g_ref, other in zip(halves, g_refs, _beside(c_ref, layer, count)):
            g = half * (c + other)
            diagonal = diagonal + g
            _store(g_ref, layer, g)
        if ends:
            diagonal = jnp.where(c > 0, diagonal, 1.0)
        inverse = pl.reciprocal(diagonal, approx=True)
        inverse = inverse * (2.0 - diagonal * inverse)
        inverse = inverse * (2.0 - diagonal * inverse)
        weight = WEIGHT * inverse
        _store(w_ref, layer, weight)
        _store(u1_ref, layer, weight * _load(f_ref, layer, count))

    _chunks(lo, hi, STEP, faces)
    lo, hi = lo + 1, hi - 1

    def second(layer, count):
        pulled = _pull(u1_ref, g_refs, gz_ref, layer, count)
        f = _load(f_ref, layer, count)
        _store(u2_ref, layer, _load(w_ref, layer, count) * ((2.0 - WEIGHT) * f + pulled))
        if t_ref is not None:
            _store(t_ref, layer, (1.0 - WEIGHT) ** 2 * f - WEIGHT * pulled)

    _chunks(lo, hi, STEP, second)


def _pull(u_ref, g_refs, gz_ref, layer, count):
    total = _load(gz_ref, layer, count) * _load(u_ref, layer + 1, count)
    total = total + _load(gz_ref, layer - 1, count) * _load(u_ref, layer - 1, count)
    for g_ref, other in zip(g_refs, _beside(u_ref, layer, count)):
        total = total + _load(g_ref, layer, count) * other
    return total


def _residual(u2_ref, t_ref, g_refs, gz_ref, pair_ref, lo, hi, pair_at):
    def body(layer, count):
        left = _load(t_ref, layer, count) + _pull(u2_ref, g_refs, gz_ref, layer, count)
        pairs = left.reshape(count // 2, 2, SUB, LANES)
        _store(pair_ref, (layer - lo) // 2 + pair_at, pairs[:, 0] + pairs[:, 1])

    _chunks(lo, hi, STEP, body)


def _pooled(pair_ref, rows):
    lane, to = _iota((LANES, LANES), 0), _iota((LANES, LANES), 1)
    place = (lane // 64) * 16 + (lane % 32) // 2
    total = jnp.zeros((rows, LANES), F32)
    for k in range(4):
        part = pair_ref[pl.ds(k, rows, stride=4), :]
        pick = jnp.where(to == place + 32 * k, 0.125, 0.0).astype(BF16)
        high = part.astype(BF16)
        rest = part - high.astype(F32)
        low = rest.astype(BF16)
        lowest = (rest - low.astype(F32)).astype(BF16)
        for term in (high, low, lowest):
            total = total + jnp.dot(term, pick, preferred_element_type=F32)
    return total


def edges_kernel(layers, f_in, c_in, first_ref, last_ref, f_held, c_held, f_ref, c_ref, sems):
    def layer_of(row):
        return jnp.where(row < SIDE, row, row + layers - 2 * SIDE)

    copies = [
        pltpu.make_async_copy(cells, held, sems.at[at])
        for at, (cells, held) in enumerate(((f_in, f_held), (c_in, c_held)))
    ]
    for copy in copies:
        copy.start()
    rows = SIDE * SUB
    for at, (copy, held, ref) in enumerate(zip(copies, (f_held, c_held), (f_ref, c_ref))):
        copy.wait()
        _transposed(held, ref, layer_of, 2 * SIDE)
        first_ref[at * rows : (at + 1) * rows, :] = ref[:rows, :].astype(BF16)
        last_ref[at * rows : (at + 1) * rows, :] = ref[rows:, :].astype(BF16)


def _halo(side_ref, at, last):
    rows = SIDE * SUB
    cells = side_ref[at * rows : (at + 1) * rows, :].astype(F32)
    return cells[rows - HALO * SUB :] if last else cells[: HALO * SUB]


def inner_kernel(layers, f_in, c_in, near_ref, u2_ref, c_ref, f_ref, *work):
    for cells, ref in ((f_in, f_ref), (c_in, c_ref)):
        _transposed(cells, ref, lambda row: row, layers)
    rows = (EDGE + HALO) * SUB
    for at, ref in enumerate((f_ref, c_ref)):
        near_ref[2 * at * rows : (2 * at + 1) * rows, :] = ref[:rows, :]
        near_ref[(2 * at + 1) * rows : (2 * at + 2) * rows, :] = ref[layers * SUB - rows :, :]
    *g, gz, w, u1 = work
    _sweeps(c_ref, f_ref, g, gz, w, u1, u2_ref, None, EDGE + 1, layers - EDGE - 1, False)
    u2_ref[: EDGE * SUB, :] = jnp.zeros((EDGE * SUB, LANES), F32)
    u2_ref[(layers - EDGE) * SUB : layers * SUB, :] = jnp.zeros((EDGE * SUB, LANES), F32)


def outer_kernel(layers, box_rows, boxes, owner_ref, before_ref, after_ref, near_ref, u2_in, slots_ref, c_ref, f_ref, *work):
    *g, gz, w, u1, u2, settled_ref, mixed_ref = work
    span = EDGE + 2 * HALO
    total = 2 * span
    halo, own = HALO * SUB, (EDGE + HALO) * SUB
    for at, ref in enumerate((f_ref, c_ref)):
        ref[:halo, :] = _halo(before_ref, at, True)
        ref[halo : span * SUB, :] = near_ref[2 * at * own : (2 * at + 1) * own, :]
        ref[span * SUB : total * SUB - halo, :] = near_ref[(2 * at + 1) * own : (2 * at + 2) * own, :]
        ref[total * SUB - halo :, :] = _halo(after_ref, at, False)
    _sweeps(c_ref, f_ref, g, gz, w, u1, u2, None, HALO, total - HALO, True)

    rows = layers * SUB
    edge = EDGE * SUB
    settled_ref[edge : rows - edge, :] = u2_in[edge : rows - edge, :]
    settled_ref[:edge, :] = u2[halo : halo + edge, :]
    settled_ref[rows - edge :, :] = u2[span * SUB + halo : span * SUB + halo + edge, :]
    slots_ref[...] = jnp.zeros(slots_ref.shape, BF16)
    for k in range(boxes):
        owner = owner_ref[k]
        seen = jnp.int32(0)
        for j in range(k):
            seen = jnp.where(owner_ref[j] == owner, 1, seen)
        second = jnp.int32(-1)
        for j in range(k + 1, boxes):
            second = jnp.where(owner_ref[j] == owner, j, second)

        @pl.when(seen == 0)
        def _():
            mixed_ref[pl.ds(0, box_rows, stride=2), :] = settled_ref[k * box_rows : (k + 1) * box_rows, :]

            @pl.when(second < 0)
            def _():
                mixed_ref[pl.ds(1, box_rows, stride=2), :] = jnp.zeros((box_rows, LANES), F32)

            @pl.when(second >= 0)
            def _():
                start = pl.multiple_of(jnp.maximum(second, 0) * box_rows, box_rows)
                mixed_ref[pl.ds(1, box_rows, stride=2), :] = settled_ref[pl.ds(start, box_rows), :]

            slots_ref[owner] = mixed_ref[...].astype(BF16)


def coarse_kernel(layers, before_ref, after_ref, f_in, c_in, coarse_ref, c_ref, f_ref, *work):
    *g, gz, w, u1, t, u2, pair = work
    halo, rows = HALO * SUB, layers * SUB
    for at, (cells, ref) in enumerate(((f_in, f_ref), (c_in, c_ref))):
        _transposed(cells, ref, lambda row: row, layers, HALO)
        ref[:halo, :] = _halo(before_ref, at, True)
        ref[halo + rows :, :] = _halo(after_ref, at, False)
    _sweeps(c_ref, f_ref, g, gz, w, u1, u2, t, HALO, HALO + layers, True)
    _residual(u2, t, g, gz, pair, HALO, HALO + layers, 0)
    rows = coarse_ref.shape[0] - 16
    means = _pooled(pair, rows)
    peak = jnp.full((16, LANES), jnp.max(jnp.abs(means)), F32)
    power = jnp.floor(jnp.log2(jnp.clip(peak, 1e-30, 1e30)))
    coarse_ref[:rows, :] = means * jnp.exp2(-power)[:1, :]
    coarse_ref[rows:, :] = power


def spread_kernel(sizes, block_rows, box_rows, boxes, in_ref, out_ref, mixed_ref):
    step = pl.program_id(0)
    x_count, y_count, core_count = sizes
    row = 0
    for d in range(8):
        device = step * 8 + d
        core, y, x = device % core_count, device // core_count % y_count, device // core_count // y_count
        start = ((y * core_count + core) * x_count + x) * block_rows
        power = in_ref[pl.ds(pl.multiple_of(start + boxes * box_rows, 16), 16), :]
        scale = jnp.exp2(power)[:1, :]
        for k in range(boxes):
            part = in_ref[pl.ds(pl.multiple_of(start + k * box_rows, 16), box_rows), :]
            mixed_ref[row * box_rows : (row + 1) * box_rows, :] = part * scale
            row += 1
    for group in range(row // 8):
        for lane in range(box_rows):
            tile = mixed_ref[pl.ds(group * 8 * box_rows + lane, 8, stride=box_rows), :]
            out_ref[group * 8 : (group + 1) * 8, lane * LANES : (lane + 1) * LANES] = tile


def _params(limit=VMEM_LIMIT):
    return pltpu.CompilerParams(vmem_limit_bytes=limit)


def _whole(count):
    return [pl.BlockSpec(memory_space=pltpu.VMEM)] * count


def _scratch(layers, count):
    return [pltpu.VMEM((layers * SUB, LANES), F32)] * count


def shards(sizes, source, conductivity, new_owner):
    layers, rows_y, rows_x = source.shape
    boxes = new_owner.shape[2]
    depth = layers // boxes
    group_count = lax.axis_size("grp")
    box_rows = depth * SUB
    coarse_rows = depth * SUB * LANES // 8 // LANES
    inner_boxes = boxes - 2
    f_in = jnp.transpose(source, (1, 2, 0)).reshape(rows_y * rows_x, layers)
    c_in = jnp.transpose(conductivity, (1, 2, 0)).reshape(rows_y * rows_x, layers)
    owners = new_owner.reshape(boxes)

    edge = jax.ShapeDtypeStruct((2 * SIDE * SUB, LANES), BF16)
    held = jax.ShapeDtypeStruct(f_in.shape, BF16)
    first, last, f_held, c_held = pl.pallas_call(
        functools.partial(edges_kernel, layers),
        out_shape=[edge, edge, held, held],
        in_specs=[pl.BlockSpec(memory_space=pltpu.HBM)] * 2,
        out_specs=_whole(4),
        scratch_shapes=_scratch(2 * SIDE, 2) + [pltpu.SemaphoreType.DMA((2,))],
        compiler_params=_params(),
        cost_estimate=pl.CostEstimate(flops=10**7, bytes_accessed=10**6, transcendentals=0),
        name="edge_layers",
    )(*(pltpu.with_memory_space_constraint(cells, pltpu.HBM) for cells in (f_in, c_in)))
    everyone = ("x", "y", "core", "grp")
    count = lax.axis_size(everyone)
    before = lax.ppermute(last, everyone, [(i, i + 1) for i in range(count - 1)])
    after = lax.ppermute(first, everyone, [(i + 1, i) for i in range(count - 1)])

    near, u2 = pl.pallas_call(
        functools.partial(inner_kernel, layers),
        out_shape=[
            jax.ShapeDtypeStruct((4 * (EDGE + HALO) * SUB, LANES), F32),
            jax.ShapeDtypeStruct((layers * SUB, LANES), F32),
        ],
        in_specs=_whole(2),
        out_specs=_whole(2),
        scratch_shapes=_scratch(layers, 9),
        compiler_params=_params(),
        cost_estimate=pl.CostEstimate(flops=10**8, bytes_accessed=10**7, transcendentals=0),
        name="inner_layers",
    )(f_held, c_held)

    total = 2 * (EDGE + 2 * HALO)
    slots = pl.pallas_call(
        functools.partial(outer_kernel, layers, box_rows, boxes),
        out_shape=jax.ShapeDtypeStruct((group_count, 2 * box_rows, LANES), BF16),
        in_specs=[pl.BlockSpec(memory_space=pltpu.SMEM)] + _whole(4),
        out_specs=pl.BlockSpec(memory_space=pltpu.VMEM),
        scratch_shapes=_scratch(total, 10) + _scratch(layers, 1) + _scratch(2 * depth, 1),
        compiler_params=_params(),
        name="outer_layers",
    )(owners, before, after, near, u2)

    coarse = pl.pallas_call(
        functools.partial(coarse_kernel, layers),
        out_shape=jax.ShapeDtypeStruct((boxes * coarse_rows + 16, LANES), F32),
        in_specs=_whole(4),
        out_specs=pl.BlockSpec(memory_space=pltpu.VMEM),
        scratch_shapes=_scratch(layers + 2 * HALO, 11) + _scratch(layers // 2, 1),
        compiler_params=_params(),
        cost_estimate=pl.CostEstimate(flops=10**8, bytes_accessed=10**7, transcendentals=0),
        name="coarse_rows",
    )(before, after, f_held, c_held)

    correction = lax.all_to_all(slots, "grp", split_axis=0, concat_axis=0, tiled=True)
    correction = correction.reshape(group_count, box_rows, 2, LANES).transpose(0, 2, 1, 3)
    gathered = coarse.astype(F16)
    for axes in ("x", ("y", "core")):
        gathered = lax.all_gather(gathered, axes, axis=0, tiled=True)

    devices = sizes[0] * sizes[1] * sizes[2]
    coarse_all = pl.pallas_call(
        functools.partial(spread_kernel, sizes, coarse.shape[0], coarse_rows, boxes),
        out_shape=jax.ShapeDtypeStruct((devices * boxes, coarse_rows * LANES), F32),
        grid=(devices // 8,),
        in_specs=_whole(1),
        out_specs=pl.BlockSpec((8 * boxes, coarse_rows * LANES), lambda i: (i, 0)),
        scratch_shapes=[pltpu.VMEM((8 * boxes * coarse_rows, LANES), F32)],
        compiler_params=_params(),
        name="spread_coarse",
    )(gathered.astype(F32))
    return (
        correction.reshape(1, 1, group_count, 2, box_rows * LANES),
        coarse_all[None],
    )


def solution(mesh):
    sizes = (4, 8, 2) if mesh.shape["box"] == 64 else (1, 8, 2)
    fine = Mesh(mesh.devices.reshape(sizes + (mesh.shape["grp"],)), ("x", "y", "core", "grp"))
    box = ("x", "y", "core")
    return jax.shard_map(
        functools.partial(shards, sizes),
        mesh=fine,
        in_specs=(
            P(box + ("grp",), None, None),
            P(box + ("grp",), None, None),
            P(box, "grp", None, None),
        ),
        out_specs=(P(box, "grp", None, None, None), P("grp", None, None)),
        check_vma=False,
    )
```

```python
import functools

import jax
import jax.numpy as jnp
from jax import lax
from jax.experimental import pallas as pl
from jax.experimental.pallas import tpu as pltpu
from jax.sharding import Mesh, PartitionSpec as P

WEIGHT = 0.8
F32, BF16, F16 = jnp.float32, jnp.bfloat16, jnp.float16
HALO = 3
STEP = 40
EDGE = 2
SIDE = 4
SUB, LANES = 8, 128
VMEM_LIMIT = 40 * 1024 * 1024


def _iota(shape, dim):
    return lax.broadcasted_iota(jnp.int32, shape, dim)


def _chunks(lo, hi, step, body):
    whole = (hi - lo) // step
    if whole:

        @pl.loop(0, whole)
        def _(i):
            body(lo + i * step, step)

    if lo + whole * step < hi:
        body(lo + whole * step, hi - lo - whole * step)


def _load(ref, layer, count, shift=0):
    if isinstance(layer, int):
        rows = ref[layer * SUB + shift : (layer + count) * SUB + shift, :]
    elif shift:
        rows = ref[pl.ds(layer * SUB + shift, count * SUB), :]
    else:
        rows = ref[pl.ds(pl.multiple_of(layer * SUB, SUB), count * SUB), :]
    return rows.reshape(count, SUB, LANES)


def _store(ref, layer, value):
    count = value.shape[0]
    rows = value.reshape(count * SUB, LANES)
    if isinstance(layer, int):
        ref[layer * SUB : (layer + count) * SUB, :] = rows
    else:
        ref[pl.ds(pl.multiple_of(layer * SUB, SUB), count * SUB), :] = rows


def _beside(ref, layer, count):
    here = _load(ref, layer, count)
    lane = _iota((1, SUB, LANES), 2)
    below = jnp.where(lane < 32, _load(ref, layer, count, 1), here)
    above = jnp.where(lane >= 96, _load(ref, layer, count, -1), here)
    return (
        pltpu.roll(here, LANES - 1, 2),
        pltpu.roll(here, 1, 2),
        pltpu.roll(below, LANES - 32, 2),
        pltpu.roll(above, 32, 2),
    )


def _transposed(cells_ref, out_ref, layer_of, layers, at=0):
    total = cells_ref.shape[1]
    pick = (_iota((layers, total), 1) == layer_of(_iota((layers, total), 0))).astype(BF16)
    for j in range(SUB):
        part = lax.dot_general(
            pick,
            cells_ref[j * LANES : (j + 1) * LANES, :],
            (((1,), (1,)), ((), ())),
            preferred_element_type=F32,
        )
        out_ref[pl.ds(at * SUB + j, layers, stride=SUB), :] = part


def _sweeps(c_ref, f_ref, g_refs, gz_ref, w_ref, u1_ref, u2_ref, t_ref, lo, hi, ends):
    lo, hi = lo - 2, hi + 2
    sub, lane = _iota((1, SUB, LANES), 1), _iota((1, SUB, LANES), 2)
    x, y = lane & 31, sub * 4 + (lane >> 5)
    sides = (x == 31, x == 0, y == 31, y == 0)
    halves = [jnp.where(side, 0.0, 0.5) for side in sides]
    outer = sum(side.astype(F32) for side in sides)

    def faces(layer, count):
        c = _load(c_ref, layer, count)
        after, before = _load(c_ref, layer + 1, count), _load(c_ref, layer - 1, count)
        gz, gz_before = 0.5 * (c + after), 0.5 * (c + before)
        diagonal = c * outer
        if ends:
            diagonal = diagonal + jnp.where(after > 0, gz, c) + jnp.where(before > 0, gz_before, c)
            gz = jnp.where((c > 0) & (after > 0), gz, 0.0)
        else:
            diagonal = diagonal + (gz + gz_before)
        _store(gz_ref, layer, gz)
        for half, g_ref, other in zip(halves, g_refs, _beside(c_ref, layer, count)):
            g = half * (c + other)
            diagonal = diagonal + g
            _store(g_ref, layer, g)
        if ends:
            diagonal = jnp.where(c > 0, diagonal, 1.0)
        inverse = pl.reciprocal(diagonal, approx=True)
        inverse = inverse * (2.0 - diagonal * inverse)
        inverse = inverse * (2.0 - diagonal * inverse)
        weight = WEIGHT * inverse
        _store(w_ref, layer, weight)
        _store(u1_ref, layer, weight * _load(f_ref, layer, count))

    _chunks(lo, hi, STEP, faces)
    lo, hi = lo + 1, hi - 1

    def second(layer, count):
        pulled = _pull(u1_ref, g_refs, gz_ref, layer, count)
        f = _load(f_ref, layer, count)
        _store(u2_ref, layer, _load(w_ref, layer, count) * ((2.0 - WEIGHT) * f + pulled))
        if t_ref is not None:
            _store(t_ref, layer, (1.0 - WEIGHT) ** 2 * f - WEIGHT * pulled)

    _chunks(lo, hi, STEP, second)


def _pull(u_ref, g_refs, gz_ref, layer, count):
    total = _load(gz_ref, layer, count) * _load(u_ref, layer + 1, count)
    total = total + _load(gz_ref, layer - 1, count) * _load(u_ref, layer - 1, count)
    for g_ref, other in zip(g_refs, _beside(u_ref, layer, count)):
        total = total + _load(g_ref, layer, count) * other
    return total


def _residual(u2_ref, t_ref, g_refs, gz_ref, pair_ref, lo, hi, pair_at):
    def body(layer, count):
        left = _load(t_ref, layer, count) + _pull(u2_ref, g_refs, gz_ref, layer, count)
        pairs = left.reshape(count // 2, 2, SUB, LANES)
        _store(pair_ref, (layer - lo) // 2 + pair_at, pairs[:, 0] + pairs[:, 1])

    _chunks(lo, hi, STEP, body)


def _pooled(pair_ref, rows):
    lane, to = _iota((LANES, LANES), 0), _iota((LANES, LANES), 1)
    place = (lane // 64) * 16 + (lane % 32) // 2
    total = jnp.zeros((rows, LANES), F32)
    for k in range(4):
        part = pair_ref[pl.ds(k, rows, stride=4), :]
        pick = jnp.where(to == place + 32 * k, 0.125, 0.0).astype(BF16)
        high = part.astype(BF16)
        rest = part - high.astype(F32)
        low = rest.astype(BF16)
        lowest = (rest - low.astype(F32)).astype(BF16)
        for term in (high, low, lowest):
            total = total + jnp.dot(term, pick, preferred_element_type=F32)
    return total


def edges_kernel(layers, f_in, c_in, first_ref, last_ref, f_held, c_held, f_ref, c_ref, sems):
    def layer_of(row):
        return jnp.where(row < SIDE, row, row + layers - 2 * SIDE)

    copies = [
        pltpu.make_async_copy(cells, held, sems.at[at])
        for at, (cells, held) in enumerate(((f_in, f_held), (c_in, c_held)))
    ]
    for copy in copies:
        copy.start()
    rows = SIDE * SUB
    for at, (copy, held, ref) in enumerate(zip(copies, (f_held, c_held), (f_ref, c_ref))):
        copy.wait()
        _transposed(held, ref, layer_of, 2 * SIDE)
        first_ref[at * rows : (at + 1) * rows, :] = ref[:rows, :].astype(BF16)
        last_ref[at * rows : (at + 1) * rows, :] = ref[rows:, :].astype(BF16)


def _halo(side_ref, at, last):
    rows = SIDE * SUB
    cells = side_ref[at * rows : (at + 1) * rows, :].astype(F32)
    return cells[rows - HALO * SUB :] if last else cells[: HALO * SUB]


def inner_kernel(layers, f_in, c_in, near_ref, u2_ref, c_ref, f_ref, *work):
    for cells, ref in ((f_in, f_ref), (c_in, c_ref)):
        _transposed(cells, ref, lambda row: row, layers)
    rows = (EDGE + HALO) * SUB
    for at, ref in enumerate((f_ref, c_ref)):
        near_ref[2 * at * rows : (2 * at + 1) * rows, :] = ref[:rows, :]
        near_ref[(2 * at + 1) * rows : (2 * at + 2) * rows, :] = ref[layers * SUB - rows :, :]
    *g, gz, w, u1 = work
    _sweeps(c_ref, f_ref, g, gz, w, u1, u2_ref, None, EDGE + 1, layers - EDGE - 1, False)
    u2_ref[: EDGE * SUB, :] = jnp.zeros((EDGE * SUB, LANES), F32)
    u2_ref[(layers - EDGE) * SUB : layers * SUB, :] = jnp.zeros((EDGE * SUB, LANES), F32)


def outer_kernel(layers, box_rows, boxes, owner_in, before_ref, after_ref, near_ref, u2_in, slots_ref, c_ref, f_ref, *work):
    *g, gz, w, u1, u2, settled_ref, mixed_ref, staged_ref, owner_ref, owner_sem, sems = work
    load = pltpu.make_async_copy(owner_in, owner_ref, owner_sem.at[0])
    load.start()
    span = EDGE + 2 * HALO
    total = 2 * span
    halo, own = HALO * SUB, (EDGE + HALO) * SUB
    for at, ref in enumerate((f_ref, c_ref)):
        ref[:halo, :] = _halo(before_ref, at, True)
        ref[halo : span * SUB, :] = near_ref[2 * at * own : (2 * at + 1) * own, :]
        ref[span * SUB : total * SUB - halo, :] = near_ref[(2 * at + 1) * own : (2 * at + 2) * own, :]
        ref[total * SUB - halo :, :] = _halo(after_ref, at, False)
    _sweeps(c_ref, f_ref, g, gz, w, u1, u2, None, HALO, total - HALO, True)
    rows = layers * SUB
    edge = EDGE * SUB
    settled_ref[edge : rows - edge, :] = u2_in[edge : rows - edge, :]
    settled_ref[:edge, :] = u2[halo : halo + edge, :]
    settled_ref[rows - edge :, :] = u2[span * SUB + halo : span * SUB + halo + edge, :]
    load.wait()

    owners = [owner_ref[0, k] for k in range(boxes)]
    sends = []
    for owner in range(slots_ref.shape[0]):
        first, second = jnp.int32(-1), jnp.int32(-1)
        for k in range(boxes):
            named = owners[k] == owner
            second = jnp.where(named & (first >= 0), k, second)
            first = jnp.where(named & (first < 0), k, first)

        @pl.when(first < 0)
        def _():
            staged_ref[owner] = jnp.zeros((2 * box_rows, LANES), BF16)

        @pl.when(first >= 0)
        def _():
            for rank, box in enumerate((first, second)):
                start = pl.multiple_of(jnp.maximum(box, 0) * box_rows, box_rows)
                cells = settled_ref[pl.ds(start, box_rows), :]
                mixed_ref[pl.ds(rank, box_rows, stride=2), :] = cells if rank == 0 else jnp.where(box >= 0, cells, 0.0)
            staged_ref[owner] = mixed_ref[...].astype(BF16)

        sends.append(pltpu.make_async_copy(staged_ref.at[owner], slots_ref.at[owner], sems.at[owner]))
        sends[-1].start()
    for send in sends:
        send.wait()


def coarse_kernel(layers, before_ref, after_ref, f_in, c_in, coarse_ref, c_ref, f_ref, *work):
    *g, gz, w, u1, t, u2, pair = work
    halo, rows = HALO * SUB, layers * SUB
    for at, (cells, ref) in enumerate(((f_in, f_ref), (c_in, c_ref))):
        _transposed(cells, ref, lambda row: row, layers, HALO)
        ref[:halo, :] = _halo(before_ref, at, True)
        ref[halo + rows :, :] = _halo(after_ref, at, False)
    _sweeps(c_ref, f_ref, g, gz, w, u1, u2, t, HALO, HALO + layers, True)
    _residual(u2, t, g, gz, pair, HALO, HALO + layers, 0)
    rows = coarse_ref.shape[0] - 16
    means = _pooled(pair, rows)
    peak = jnp.full((16, LANES), jnp.max(jnp.abs(means)), F32)
    power = jnp.floor(jnp.log2(jnp.clip(peak, 1e-30, 1e30)))
    coarse_ref[:rows, :] = means * jnp.exp2(-power)[:1, :]
    coarse_ref[rows:, :] = power


def spread_kernel(sizes, block_rows, box_rows, boxes, in_ref, out_ref):
    step = pl.program_id(0)
    x_count, y_count, core_count = sizes
    parts = []
    for d in range(8):
        device = step * 8 + d
        core, y, x = device % core_count, device // core_count % y_count, device // core_count // y_count
        start = ((y * core_count + core) * x_count + x) * block_rows
        power = in_ref[pl.ds(pl.multiple_of(start + boxes * box_rows, 16), 16), :]
        scale = jnp.exp2(power)[:1, :]
        for k in range(boxes):
            parts.append(in_ref[pl.ds(pl.multiple_of(start + k * box_rows, 16), box_rows), :] * scale)
    for at in range(0, len(parts), 8):
        tiles = jnp.swapaxes(jnp.stack(parts[at : at + 8]), 0, 1)
        for lane in range(box_rows):
            out_ref[at : at + 8, lane * LANES : (lane + 1) * LANES] = tiles[lane]


def _params(limit=VMEM_LIMIT):
    return pltpu.CompilerParams(vmem_limit_bytes=limit)


def _whole(count):
    return [pl.BlockSpec(memory_space=pltpu.VMEM)] * count


def _scratch(layers, count):
    return [pltpu.VMEM((layers * SUB, LANES), F32)] * count


def shards(sizes, source, conductivity, new_owner):
    layers, rows_y, rows_x = source.shape
    boxes = new_owner.shape[2]
    depth = layers // boxes
    group_count = lax.axis_size("grp")
    box_rows = depth * SUB
    coarse_rows = depth * SUB * LANES // 8 // LANES
    inner_boxes = boxes - 2
    f_in = jnp.transpose(source, (1, 2, 0)).reshape(rows_y * rows_x, layers)
    c_in = jnp.transpose(conductivity, (1, 2, 0)).reshape(rows_y * rows_x, layers)
    owners = new_owner.reshape(1, boxes)

    edge = jax.ShapeDtypeStruct((2 * SIDE * SUB, LANES), BF16)
    held = jax.ShapeDtypeStruct(f_in.shape, BF16)
    first, last, f_held, c_held = pl.pallas_call(
        functools.partial(edges_kernel, layers),
        out_shape=[edge, edge, held, held],
        in_specs=[pl.BlockSpec(memory_space=pltpu.HBM)] * 2,
        out_specs=_whole(4),
        scratch_shapes=_scratch(2 * SIDE, 2) + [pltpu.SemaphoreType.DMA((2,))],
        compiler_params=_params(),
        cost_estimate=pl.CostEstimate(flops=10**7, bytes_accessed=10**6, transcendentals=0),
        name="edge_layers",
    )(*(pltpu.with_memory_space_constraint(cells, pltpu.HBM) for cells in (f_in, c_in)))
    everyone = ("x", "y", "core", "grp")
    count = lax.axis_size(everyone)
    before = lax.ppermute(last, everyone, [(i, i + 1) for i in range(count - 1)])
    after = lax.ppermute(first, everyone, [(i + 1, i) for i in range(count - 1)])

    near, u2 = pl.pallas_call(
        functools.partial(inner_kernel, layers),
        out_shape=[
            jax.ShapeDtypeStruct((4 * (EDGE + HALO) * SUB, LANES), F32),
            jax.ShapeDtypeStruct((layers * SUB, LANES), F32),
        ],
        in_specs=_whole(2),
        out_specs=_whole(2),
        scratch_shapes=_scratch(layers, 9),
        compiler_params=_params(),
        cost_estimate=pl.CostEstimate(flops=10**8, bytes_accessed=10**7, transcendentals=0),
        name="inner_layers",
    )(f_held, c_held)

    total = 2 * (EDGE + 2 * HALO)
    slots_shape = (group_count, 2 * box_rows, LANES)
    slots = pl.pallas_call(
        functools.partial(outer_kernel, layers, box_rows, boxes),
        out_shape=jax.ShapeDtypeStruct(slots_shape, BF16),
        in_specs=[pl.BlockSpec(memory_space=pltpu.HBM)] + _whole(4),
        out_specs=pl.BlockSpec(memory_space=pltpu.HBM),
        scratch_shapes=_scratch(total, 10)
        + _scratch(layers, 1)
        + _scratch(2 * depth, 1)
        + [
            pltpu.VMEM(slots_shape, BF16),
            pltpu.SMEM((1, boxes), jnp.int32),
            pltpu.SemaphoreType.DMA((1,)),
            pltpu.SemaphoreType.DMA((group_count,)),
        ],
        compiler_params=_params(),
        name="outer_layers",
    )(pltpu.with_memory_space_constraint(owners, pltpu.HBM), before, after, near, u2)

    coarse = pl.pallas_call(
        functools.partial(coarse_kernel, layers),
        out_shape=jax.ShapeDtypeStruct((boxes * coarse_rows + 16, LANES), F32),
        in_specs=_whole(4),
        out_specs=pl.BlockSpec(memory_space=pltpu.VMEM),
        scratch_shapes=_scratch(layers + 2 * HALO, 11) + _scratch(layers // 2, 1),
        compiler_params=_params(),
        cost_estimate=pl.CostEstimate(flops=10**8, bytes_accessed=10**7, transcendentals=0),
        name="coarse_rows",
    )(before, after, f_held, c_held)

    correction = lax.all_to_all(slots, "grp", split_axis=0, concat_axis=0, tiled=True)
    correction = correction.reshape(group_count, box_rows, 2, LANES).transpose(0, 2, 1, 3)
    gathered = coarse.astype(F16)
    for axes in ("x", ("y", "core")):
        gathered = lax.all_gather(gathered, axes, axis=0, tiled=True)

    devices = sizes[0] * sizes[1] * sizes[2]
    coarse_all = pl.pallas_call(
        functools.partial(spread_kernel, sizes, coarse.shape[0], coarse_rows, boxes),
        out_shape=jax.ShapeDtypeStruct((devices * boxes, coarse_rows * LANES), F32),
        grid=(devices // 8,),
        in_specs=_whole(1),
        out_specs=pl.BlockSpec((8 * boxes, coarse_rows * LANES), lambda i: (i, 0)),
        compiler_params=_params(),
        name="spread_coarse",
    )(gathered.astype(F32))
    return (
        correction.reshape(1, 1, group_count, 2, box_rows * LANES),
        coarse_all[None],
    )


def solution(mesh):
    sizes = (4, 8, 2) if mesh.shape["box"] == 64 else (1, 8, 2)
    fine = Mesh(mesh.devices.reshape(sizes + (mesh.shape["grp"],)), ("x", "y", "core", "grp"))
    box = ("x", "y", "core")
    return jax.shard_map(
        functools.partial(shards, sizes),
        mesh=fine,
        in_specs=(
            P(box + ("grp",), None, None),
            P(box + ("grp",), None, None),
            P(box, "grp", None, None),
        ),
        out_specs=(P(box, "grp", None, None, None), P("grp", None, None)),
        check_vma=False,
    )
```

```python
import functools

import jax
import jax.numpy as jnp
from jax import lax
from jax.experimental import pallas as pl
from jax.experimental.pallas import tpu as pltpu
from jax.sharding import Mesh, PartitionSpec as P

WEIGHT = 0.8
F32, BF16, F16 = jnp.float32, jnp.bfloat16, jnp.float16
HALO = 3
STEP = 40
EDGE = 2
SIDE = 4
SUB, LANES = 8, 128
VMEM_LIMIT = 40 * 1024 * 1024


def _iota(shape, dim):
    return lax.broadcasted_iota(jnp.int32, shape, dim)


def _chunks(lo, hi, step, body):
    whole = (hi - lo) // step
    if whole:

        @pl.loop(0, whole)
        def _(i):
            body(lo + i * step, step)

    if lo + whole * step < hi:
        body(lo + whole * step, hi - lo - whole * step)


def _load(ref, layer, count, shift=0):
    if isinstance(layer, int):
        rows = ref[layer * SUB + shift : (layer + count) * SUB + shift, :]
    elif shift:
        rows = ref[pl.ds(layer * SUB + shift, count * SUB), :]
    else:
        rows = ref[pl.ds(pl.multiple_of(layer * SUB, SUB), count * SUB), :]
    return rows.reshape(count, SUB, LANES)


def _store(ref, layer, value):
    count = value.shape[0]
    rows = value.reshape(count * SUB, LANES)
    if isinstance(layer, int):
        ref[layer * SUB : (layer + count) * SUB, :] = rows
    else:
        ref[pl.ds(pl.multiple_of(layer * SUB, SUB), count * SUB), :] = rows


def _beside(ref, layer, count):
    here = _load(ref, layer, count)
    lane = _iota((1, SUB, LANES), 2)
    below = jnp.where(lane < 32, _load(ref, layer, count, 1), here)
    above = jnp.where(lane >= 96, _load(ref, layer, count, -1), here)
    return (
        pltpu.roll(here, LANES - 1, 2),
        pltpu.roll(here, 1, 2),
        pltpu.roll(below, LANES - 32, 2),
        pltpu.roll(above, 32, 2),
    )


def _transposed(cells_ref, out_ref, layer_of, layers, at=0):
    total = cells_ref.shape[1]
    pick = (_iota((layers, total), 1) == layer_of(_iota((layers, total), 0))).astype(BF16)
    for j in range(SUB):
        part = lax.dot_general(
            pick,
            cells_ref[j * LANES : (j + 1) * LANES, :],
            (((1,), (1,)), ((), ())),
            preferred_element_type=F32,
        )
        out_ref[pl.ds(at * SUB + j, layers, stride=SUB), :] = part


def _sweeps(c_ref, f_ref, g_refs, gz_ref, w_ref, u1_ref, u2_ref, t_ref, lo, hi, ends):
    lo, hi = lo - 2, hi + 2
    sub, lane = _iota((1, SUB, LANES), 1), _iota((1, SUB, LANES), 2)
    x, y = lane & 31, sub * 4 + (lane >> 5)
    sides = (x == 31, x == 0, y == 31, y == 0)
    halves = [jnp.where(side, 0.0, 0.5) for side in sides]
    outer = sum(side.astype(F32) for side in sides)

    def faces(layer, count):
        c = _load(c_ref, layer, count)
        after, before = _load(c_ref, layer + 1, count), _load(c_ref, layer - 1, count)
        gz, gz_before = 0.5 * (c + after), 0.5 * (c + before)
        diagonal = c * outer
        if ends:
            diagonal = diagonal + jnp.where(after > 0, gz, c) + jnp.where(before > 0, gz_before, c)
            gz = jnp.where((c > 0) & (after > 0), gz, 0.0)
        else:
            diagonal = diagonal + (gz + gz_before)
        _store(gz_ref, layer, gz)
        for half, g_ref, other in zip(halves, g_refs, _beside(c_ref, layer, count)):
            g = half * (c + other)
            diagonal = diagonal + g
            _store(g_ref, layer, g)
        if ends:
            diagonal = jnp.where(c > 0, diagonal, 1.0)
        inverse = pl.reciprocal(diagonal, approx=True)
        inverse = inverse * (2.0 - diagonal * inverse)
        inverse = inverse * (2.0 - diagonal * inverse)
        weight = WEIGHT * inverse
        _store(w_ref, layer, weight)
        _store(u1_ref, layer, weight * _load(f_ref, layer, count))

    _chunks(lo, hi, STEP, faces)
    lo, hi = lo + 1, hi - 1

    def second(layer, count):
        pulled = _pull(u1_ref, g_refs, gz_ref, layer, count)
        f = _load(f_ref, layer, count)
        _store(u2_ref, layer, _load(w_ref, layer, count) * ((2.0 - WEIGHT) * f + pulled))
        if t_ref is not None:
            _store(t_ref, layer, (1.0 - WEIGHT) ** 2 * f - WEIGHT * pulled)

    _chunks(lo, hi, STEP, second)


def _pull(u_ref, g_refs, gz_ref, layer, count):
    total = _load(gz_ref, layer, count) * _load(u_ref, layer + 1, count)
    total = total + _load(gz_ref, layer - 1, count) * _load(u_ref, layer - 1, count)
    for g_ref, other in zip(g_refs, _beside(u_ref, layer, count)):
        total = total + _load(g_ref, layer, count) * other
    return total


def _residual(u2_ref, t_ref, g_refs, gz_ref, pair_ref, lo, hi, pair_at):
    def body(layer, count):
        left = _load(t_ref, layer, count) + _pull(u2_ref, g_refs, gz_ref, layer, count)
        pairs = left.reshape(count // 2, 2, SUB, LANES)
        _store(pair_ref, (layer - lo) // 2 + pair_at, pairs[:, 0] + pairs[:, 1])

    _chunks(lo, hi, STEP, body)


def _pooled(pair_ref, rows):
    lane, to = _iota((LANES, LANES), 0), _iota((LANES, LANES), 1)
    place = (lane // 64) * 16 + (lane % 32) // 2
    total = jnp.zeros((rows, LANES), F32)
    for k in range(4):
        part = pair_ref[pl.ds(k, rows, stride=4), :]
        pick = jnp.where(to == place + 32 * k, 0.125, 0.0).astype(BF16)
        high = part.astype(BF16)
        rest = part - high.astype(F32)
        low = rest.astype(BF16)
        lowest = (rest - low.astype(F32)).astype(BF16)
        for term in (high, low, lowest):
            total = total + jnp.dot(term, pick, preferred_element_type=F32)
    return total


def edges_kernel(layers, f_in, c_in, first_ref, last_ref, f_held, c_held, f_ref, c_ref, sems):
    def layer_of(row):
        return jnp.where(row < SIDE, row, row + layers - 2 * SIDE)

    copies = [
        pltpu.make_async_copy(cells, held, sems.at[at])
        for at, (cells, held) in enumerate(((f_in, f_held), (c_in, c_held)))
    ]
    for copy in copies:
        copy.start()
    rows = SIDE * SUB
    for at, (copy, held, ref) in enumerate(zip(copies, (f_held, c_held), (f_ref, c_ref))):
        copy.wait()
        _transposed(held, ref, layer_of, 2 * SIDE)
        first_ref[at * rows : (at + 1) * rows, :] = ref[:rows, :].astype(BF16)
        last_ref[at * rows : (at + 1) * rows, :] = ref[rows:, :].astype(BF16)


def _halo(side_ref, at, last):
    rows = SIDE * SUB
    cells = side_ref[at * rows : (at + 1) * rows, :].astype(F32)
    return cells[rows - HALO * SUB :] if last else cells[: HALO * SUB]


def inner_kernel(layers, f_in, c_in, near_ref, u2_ref, slots_ref, c_ref, f_ref, *work):
    *g, gz, w, u1, blank_ref, sems = work
    blank_ref[...] = jnp.zeros(blank_ref.shape, BF16)
    blanks = [pltpu.make_async_copy(blank_ref, slots_ref.at[i], sems.at[i]) for i in range(slots_ref.shape[0])]
    for copy in blanks:
        copy.start()
    for cells, ref in ((f_in, f_ref), (c_in, c_ref)):
        _transposed(cells, ref, lambda row: row, layers)
    rows = (EDGE + HALO) * SUB
    for at, ref in enumerate((f_ref, c_ref)):
        near_ref[2 * at * rows : (2 * at + 1) * rows, :] = ref[:rows, :]
        near_ref[(2 * at + 1) * rows : (2 * at + 2) * rows, :] = ref[layers * SUB - rows :, :]
    _sweeps(c_ref, f_ref, g, gz, w, u1, u2_ref, None, EDGE + 1, layers - EDGE - 1, False)
    u2_ref[: EDGE * SUB, :] = jnp.zeros((EDGE * SUB, LANES), F32)
    u2_ref[(layers - EDGE) * SUB : layers * SUB, :] = jnp.zeros((EDGE * SUB, LANES), F32)
    for copy in blanks:
        copy.wait()


def outer_kernel(layers, box_rows, boxes, owner_in, before_ref, after_ref, near_ref, u2_in, slots_in, slots_ref, c_ref, f_ref, *work):
    del slots_in
    *g, gz, w, u1, u2, settled_ref, mixed_ref, staged_ref, owner_ref, owner_sem, sems = work
    load = pltpu.make_async_copy(owner_in, owner_ref, owner_sem.at[0])
    load.start()
    span = EDGE + 2 * HALO
    total = 2 * span
    halo, own = HALO * SUB, (EDGE + HALO) * SUB
    for at, ref in enumerate((f_ref, c_ref)):
        ref[:halo, :] = _halo(before_ref, at, True)
        ref[halo : span * SUB, :] = near_ref[2 * at * own : (2 * at + 1) * own, :]
        ref[span * SUB : total * SUB - halo, :] = near_ref[(2 * at + 1) * own : (2 * at + 2) * own, :]
        ref[total * SUB - halo :, :] = _halo(after_ref, at, False)
    _sweeps(c_ref, f_ref, g, gz, w, u1, u2, None, HALO, total - HALO, True)
    rows = layers * SUB
    edge = EDGE * SUB
    settled_ref[edge : rows - edge, :] = u2_in[edge : rows - edge, :]
    settled_ref[:edge, :] = u2[halo : halo + edge, :]
    settled_ref[rows - edge :, :] = u2[span * SUB + halo : span * SUB + halo + edge, :]
    load.wait()

    owners = [owner_ref[0, k] for k in range(boxes)]
    sends = []
    for k in range(boxes):
        first, second = jnp.int32(k), jnp.int32(-1)
        for j in range(boxes):
            if j < k:
                first = jnp.where((owners[j] == owners[k]) & (first == k), j, first)
            if j > k:
                second = jnp.where(owners[j] == owners[k], j, second)

        @pl.when(first == k)
        def _():
            mixed_ref[pl.ds(0, box_rows, stride=2), :] = settled_ref[k * box_rows : (k + 1) * box_rows, :]
            start = pl.multiple_of(jnp.maximum(second, 0) * box_rows, box_rows)
            cells = settled_ref[pl.ds(start, box_rows), :]
            mixed_ref[pl.ds(1, box_rows, stride=2), :] = jnp.where(second >= 0, cells, 0.0)
            staged_ref[k] = mixed_ref[...].astype(BF16)

        sends.append(pltpu.make_async_copy(staged_ref.at[first], slots_ref.at[owners[k]], sems.at[k]))
        sends[-1].start()
    for send in sends:
        send.wait()


def coarse_kernel(layers, before_ref, after_ref, f_in, c_in, coarse_ref, c_ref, f_ref, *work):
    *g, gz, w, u1, t, u2, pair = work
    halo, rows = HALO * SUB, layers * SUB
    for at, (cells, ref) in enumerate(((f_in, f_ref), (c_in, c_ref))):
        _transposed(cells, ref, lambda row: row, layers, HALO)
        ref[:halo, :] = _halo(before_ref, at, True)
        ref[halo + rows :, :] = _halo(after_ref, at, False)
    _sweeps(c_ref, f_ref, g, gz, w, u1, u2, t, HALO, HALO + layers, True)
    _residual(u2, t, g, gz, pair, HALO, HALO + layers, 0)
    rows = coarse_ref.shape[0] - 16
    means = _pooled(pair, rows)
    peak = jnp.full((16, LANES), jnp.max(jnp.abs(means)), F32)
    power = jnp.floor(jnp.log2(jnp.clip(peak, 1e-30, 1e30)))
    coarse_ref[:rows, :] = means * jnp.exp2(-power)[:1, :]
    coarse_ref[rows:, :] = power


def spread_kernel(sizes, block_rows, box_rows, boxes, in_ref, out_ref):
    step = pl.program_id(0)
    x_count, y_count, core_count = sizes
    parts = []
    for d in range(8):
        device = step * 8 + d
        core, y, x = device % core_count, device // core_count % y_count, device // core_count // y_count
        start = ((y * core_count + core) * x_count + x) * block_rows
        power = in_ref[pl.ds(pl.multiple_of(start + boxes * box_rows, 16), 16), :]
        scale = jnp.exp2(power)[:1, :]
        for k in range(boxes):
            parts.append(in_ref[pl.ds(pl.multiple_of(start + k * box_rows, 16), box_rows), :] * scale)
    for at in range(0, len(parts), 8):
        tiles = jnp.swapaxes(jnp.stack(parts[at : at + 8]), 0, 1)
        for lane in range(box_rows):
            out_ref[at : at + 8, lane * LANES : (lane + 1) * LANES] = tiles[lane]


def _params(limit=VMEM_LIMIT):
    return pltpu.CompilerParams(vmem_limit_bytes=limit)


def _whole(count):
    return [pl.BlockSpec(memory_space=pltpu.VMEM)] * count


def _scratch(layers, count):
    return [pltpu.VMEM((layers * SUB, LANES), F32)] * count


def shards(sizes, source, conductivity, new_owner):
    layers, rows_y, rows_x = source.shape
    boxes = new_owner.shape[2]
    depth = layers // boxes
    group_count = lax.axis_size("grp")
    box_rows = depth * SUB
    coarse_rows = depth * SUB * LANES // 8 // LANES
    inner_boxes = boxes - 2
    f_in = jnp.transpose(source, (1, 2, 0)).reshape(rows_y * rows_x, layers)
    c_in = jnp.transpose(conductivity, (1, 2, 0)).reshape(rows_y * rows_x, layers)
    owners = new_owner.reshape(1, boxes)

    edge = jax.ShapeDtypeStruct((2 * SIDE * SUB, LANES), BF16)
    held = jax.ShapeDtypeStruct(f_in.shape, BF16)
    first, last, f_held, c_held = pl.pallas_call(
        functools.partial(edges_kernel, layers),
        out_shape=[edge, edge, held, held],
        in_specs=[pl.BlockSpec(memory_space=pltpu.HBM)] * 2,
        out_specs=_whole(4),
        scratch_shapes=_scratch(2 * SIDE, 2) + [pltpu.SemaphoreType.DMA((2,))],
        compiler_params=_params(),
        cost_estimate=pl.CostEstimate(flops=10**7, bytes_accessed=10**6, transcendentals=0),
        name="edge_layers",
    )(*(pltpu.with_memory_space_constraint(cells, pltpu.HBM) for cells in (f_in, c_in)))
    everyone = ("x", "y", "core", "grp")
    count = lax.axis_size(everyone)
    before = lax.ppermute(last, everyone, [(i, i + 1) for i in range(count - 1)])
    after = lax.ppermute(first, everyone, [(i + 1, i) for i in range(count - 1)])

    slots_shape = (group_count, 2 * box_rows, LANES)
    hbm = pl.BlockSpec(memory_space=pltpu.HBM)
    near, u2, slots = pl.pallas_call(
        functools.partial(inner_kernel, layers),
        out_shape=[
            jax.ShapeDtypeStruct((4 * (EDGE + HALO) * SUB, LANES), F32),
            jax.ShapeDtypeStruct((layers * SUB, LANES), F32),
            pltpu.HBM(slots_shape, BF16),
        ],
        in_specs=_whole(2),
        out_specs=_whole(2) + [hbm],
        scratch_shapes=_scratch(layers, 9)
        + [pltpu.VMEM(slots_shape[1:], BF16), pltpu.SemaphoreType.DMA((group_count,))],
        compiler_params=_params(),
        cost_estimate=pl.CostEstimate(flops=10**8, bytes_accessed=10**7, transcendentals=0),
        name="inner_layers",
    )(f_held, c_held)

    total = 2 * (EDGE + 2 * HALO)
    slots = pl.pallas_call(
        functools.partial(outer_kernel, layers, box_rows, boxes),
        out_shape=jax.ShapeDtypeStruct(slots_shape, BF16),
        in_specs=[hbm] + _whole(4) + [hbm],
        out_specs=hbm,
        scratch_shapes=_scratch(total, 10)
        + _scratch(layers, 1)
        + _scratch(2 * depth, 1)
        + [
            pltpu.VMEM((boxes,) + slots_shape[1:], BF16),
            pltpu.SMEM((1, boxes), jnp.int32),
            pltpu.SemaphoreType.DMA((1,)),
            pltpu.SemaphoreType.DMA((boxes,)),
        ],
        input_output_aliases={5: 0},
        compiler_params=_params(),
        name="outer_layers",
    )(
        pltpu.with_memory_space_constraint(owners, pltpu.HBM),
        before,
        after,
        near,
        u2,
        pltpu.with_memory_space_constraint(slots, pltpu.HBM),
    )

    coarse = pl.pallas_call(
        functools.partial(coarse_kernel, layers),
        out_shape=jax.ShapeDtypeStruct((boxes * coarse_rows + 16, LANES), F32),
        in_specs=_whole(4),
        out_specs=pl.BlockSpec(memory_space=pltpu.VMEM),
        scratch_shapes=_scratch(layers + 2 * HALO, 11) + _scratch(layers // 2, 1),
        compiler_params=_params(),
        cost_estimate=pl.CostEstimate(flops=10**8, bytes_accessed=10**7, transcendentals=0),
        name="coarse_rows",
    )(before, after, f_held, c_held)

    correction = lax.all_to_all(slots, "grp", split_axis=0, concat_axis=0, tiled=True)
    correction = correction.reshape(group_count, box_rows, 2, LANES).transpose(0, 2, 1, 3)
    gathered = coarse.astype(F16)
    for axes in ("x", ("y", "core")):
        gathered = lax.all_gather(gathered, axes, axis=0, tiled=True)

    devices = sizes[0] * sizes[1] * sizes[2]
    coarse_all = pl.pallas_call(
        functools.partial(spread_kernel, sizes, coarse.shape[0], coarse_rows, boxes),
        out_shape=jax.ShapeDtypeStruct((devices * boxes, coarse_rows * LANES), F32),
        grid=(devices // 8,),
        in_specs=_whole(1),
        out_specs=pl.BlockSpec((8 * boxes, coarse_rows * LANES), lambda i: (i, 0)),
        compiler_params=_params(),
        name="spread_coarse",
    )(gathered.astype(F32))
    return (
        correction.reshape(1, 1, group_count, 2, box_rows * LANES),
        coarse_all[None],
    )


def solution(mesh):
    sizes = (4, 8, 2) if mesh.shape["box"] == 64 else (1, 8, 2)
    fine = Mesh(mesh.devices.reshape(sizes + (mesh.shape["grp"],)), ("x", "y", "core", "grp"))
    box = ("x", "y", "core")
    return jax.shard_map(
        functools.partial(shards, sizes),
        mesh=fine,
        in_specs=(
            P(box + ("grp",), None, None),
            P(box + ("grp",), None, None),
            P(box, "grp", None, None),
        ),
        out_specs=(P(box, "grp", None, None, None), P("grp", None, None)),
        check_vma=False,
    )
```

```python
import functools

import jax
import jax.numpy as jnp
from jax import lax
from jax.experimental import pallas as pl
from jax.experimental.pallas import tpu as pltpu
from jax.sharding import Mesh, PartitionSpec as P

WEIGHT = 0.8
F32, BF16, F16 = jnp.float32, jnp.bfloat16, jnp.float16
HALO = 3
STEP = 79
EDGE = 2
SIDE = 4
SUB, LANES = 8, 128
VMEM_LIMIT = 40 * 1024 * 1024


def _iota(shape, dim):
    return lax.broadcasted_iota(jnp.int32, shape, dim)


def _chunks(lo, hi, step, body):
    whole = (hi - lo) // step
    if whole:

        @pl.loop(0, whole)
        def _(i):
            body(lo + i * step, step)

    if lo + whole * step < hi:
        body(lo + whole * step, hi - lo - whole * step)


def _load(ref, layer, count, shift=0):
    if isinstance(layer, int):
        rows = ref[layer * SUB + shift : (layer + count) * SUB + shift, :]
    elif shift:
        rows = ref[pl.ds(layer * SUB + shift, count * SUB), :]
    else:
        rows = ref[pl.ds(pl.multiple_of(layer * SUB, SUB), count * SUB), :]
    return rows.reshape(count, SUB, LANES)


def _store(ref, layer, value):
    count = value.shape[0]
    rows = value.reshape(count * SUB, LANES)
    if isinstance(layer, int):
        ref[layer * SUB : (layer + count) * SUB, :] = rows
    else:
        ref[pl.ds(pl.multiple_of(layer * SUB, SUB), count * SUB), :] = rows


def _beside(ref, layer, count):
    here = _load(ref, layer, count)
    lane = _iota((1, SUB, LANES), 2)
    below = jnp.where(lane < 32, _load(ref, layer, count, 1), here)
    above = jnp.where(lane >= 96, _load(ref, layer, count, -1), here)
    return (
        pltpu.roll(here, LANES - 1, 2),
        pltpu.roll(here, 1, 2),
        pltpu.roll(below, LANES - 32, 2),
        pltpu.roll(above, 32, 2),
    )


def _transposed(cells_ref, out_ref, layer_of, layers, at=0):
    total = cells_ref.shape[1]
    pick = (_iota((layers, total), 1) == layer_of(_iota((layers, total), 0))).astype(BF16)
    for j in range(SUB):
        part = lax.dot_general(
            pick,
            cells_ref[j * LANES : (j + 1) * LANES, :],
            (((1,), (1,)), ((), ())),
            preferred_element_type=F32,
        )
        out_ref[pl.ds(at * SUB + j, layers, stride=SUB), :] = part


def _sweeps(c_ref, f_ref, g_refs, gz_ref, w_ref, u1_ref, u2_ref, t_ref, lo, hi, ends):
    lo, hi = lo - 2, hi + 2
    sub, lane = _iota((1, SUB, LANES), 1), _iota((1, SUB, LANES), 2)
    x, y = lane & 31, sub * 4 + (lane >> 5)
    sides = (x == 31, x == 0, y == 31, y == 0)
    halves = [jnp.where(side, 0.0, 0.5) for side in sides]
    outer = sum(side.astype(F32) for side in sides)

    def faces(layer, count):
        c = _load(c_ref, layer, count)
        after, before = _load(c_ref, layer + 1, count), _load(c_ref, layer - 1, count)
        gz, gz_before = 0.5 * (c + after), 0.5 * (c + before)
        diagonal = c * outer
        if ends:
            diagonal = diagonal + jnp.where(after > 0, gz, c) + jnp.where(before > 0, gz_before, c)
            gz = jnp.where((c > 0) & (after > 0), gz, 0.0)
        else:
            diagonal = diagonal + (gz + gz_before)
        _store(gz_ref, layer, gz)
        for half, g_ref, other in zip(halves, g_refs, _beside(c_ref, layer, count)):
            g = half * (c + other)
            diagonal = diagonal + g
            _store(g_ref, layer, g)
        if ends:
            diagonal = jnp.where(c > 0, diagonal, 1.0)
        inverse = pl.reciprocal(diagonal, approx=True)
        inverse = inverse * (2.0 - diagonal * inverse)
        inverse = inverse * (2.0 - diagonal * inverse)
        weight = WEIGHT * inverse
        _store(w_ref, layer, weight)
        _store(u1_ref, layer, weight * _load(f_ref, layer, count))

    _chunks(lo, hi, STEP, faces)
    lo, hi = lo + 1, hi - 1

    def second(layer, count):
        pulled = _pull(u1_ref, g_refs, gz_ref, layer, count)
        f = _load(f_ref, layer, count)
        _store(u2_ref, layer, _load(w_ref, layer, count) * ((2.0 - WEIGHT) * f + pulled))
        if t_ref is not None:
            _store(t_ref, layer, (1.0 - WEIGHT) ** 2 * f - WEIGHT * pulled)

    _chunks(lo, hi, STEP, second)


def _pull(u_ref, g_refs, gz_ref, layer, count):
    total = _load(gz_ref, layer, count) * _load(u_ref, layer + 1, count)
    total = total + _load(gz_ref, layer - 1, count) * _load(u_ref, layer - 1, count)
    for g_ref, other in zip(g_refs, _beside(u_ref, layer, count)):
        total = total + _load(g_ref, layer, count) * other
    return total


def _residual(u2_ref, t_ref, g_refs, gz_ref, pair_ref, lo, hi, pair_at):
    def body(layer, count):
        left = _load(t_ref, layer, count) + _pull(u2_ref, g_refs, gz_ref, layer, count)
        pairs = left.reshape(count // 2, 2, SUB, LANES)
        _store(pair_ref, (layer - lo) // 2 + pair_at, pairs[:, 0] + pairs[:, 1])

    _chunks(lo, hi, 40, body)


def _pooled(pair_ref, rows):
    lane, to = _iota((LANES, LANES), 0), _iota((LANES, LANES), 1)
    place = (lane // 64) * 16 + (lane % 32) // 2
    total = jnp.zeros((rows, LANES), F32)
    for k in range(4):
        part = pair_ref[pl.ds(k, rows, stride=4), :]
        pick = jnp.where(to == place + 32 * k, 0.125, 0.0).astype(BF16)
        high = part.astype(BF16)
        rest = part - high.astype(F32)
        low = rest.astype(BF16)
        lowest = (rest - low.astype(F32)).astype(BF16)
        for term in (high, low, lowest):
            total = total + jnp.dot(term, pick, preferred_element_type=F32)
    return total


def edges_kernel(layers, f_in, c_in, first_ref, last_ref, f_held, c_held, f_ref, c_ref, sems):
    def layer_of(row):
        return jnp.where(row < SIDE, row, row + layers - 2 * SIDE)

    copies = [
        pltpu.make_async_copy(cells, held, sems.at[at])
        for at, (cells, held) in enumerate(((f_in, f_held), (c_in, c_held)))
    ]
    for copy in copies:
        copy.start()
    rows = SIDE * SUB
    for at, (copy, held, ref) in enumerate(zip(copies, (f_held, c_held), (f_ref, c_ref))):
        copy.wait()
        _transposed(held, ref, layer_of, 2 * SIDE)
        first_ref[at * rows : (at + 1) * rows, :] = ref[:rows, :].astype(BF16)
        last_ref[at * rows : (at + 1) * rows, :] = ref[rows:, :].astype(BF16)


def _halo(side_ref, at, last):
    rows = SIDE * SUB
    cells = side_ref[at * rows : (at + 1) * rows, :].astype(F32)
    return cells[rows - HALO * SUB :] if last else cells[: HALO * SUB]


def inner_kernel(layers, f_in, c_in, near_ref, u2_ref, slots_ref, c_ref, f_ref, *work):
    *g, gz, w, u1, blank_ref, sems = work
    blank_ref[...] = jnp.zeros(blank_ref.shape, BF16)
    blanks = [pltpu.make_async_copy(blank_ref, slots_ref.at[i], sems.at[i]) for i in range(slots_ref.shape[0])]
    for copy in blanks:
        copy.start()
    for cells, ref in ((f_in, f_ref), (c_in, c_ref)):
        _transposed(cells, ref, lambda row: row, layers)
    rows = (EDGE + HALO) * SUB
    for at, ref in enumerate((f_ref, c_ref)):
        near_ref[2 * at * rows : (2 * at + 1) * rows, :] = ref[:rows, :]
        near_ref[(2 * at + 1) * rows : (2 * at + 2) * rows, :] = ref[layers * SUB - rows :, :]
    _sweeps(c_ref, f_ref, g, gz, w, u1, u2_ref, None, EDGE + 1, layers - EDGE - 1, False)
    u2_ref[: EDGE * SUB, :] = jnp.zeros((EDGE * SUB, LANES), F32)
    u2_ref[(layers - EDGE) * SUB : layers * SUB, :] = jnp.zeros((EDGE * SUB, LANES), F32)
    for copy in blanks:
        copy.wait()


def outer_kernel(layers, box_rows, boxes, owner_in, before_ref, after_ref, near_ref, u2_in, slots_in, slots_ref, c_ref, f_ref, *work):
    del slots_in
    *g, gz, w, u1, u2, settled_ref, mixed_ref, staged_ref, owner_ref, owner_sem, sems = work
    load = pltpu.make_async_copy(owner_in, owner_ref, owner_sem.at[0])
    load.start()
    span = EDGE + 2 * HALO
    total = 2 * span
    halo, own = HALO * SUB, (EDGE + HALO) * SUB
    for at, ref in enumerate((f_ref, c_ref)):
        ref[:halo, :] = _halo(before_ref, at, True)
        ref[halo : span * SUB, :] = near_ref[2 * at * own : (2 * at + 1) * own, :]
        ref[span * SUB : total * SUB - halo, :] = near_ref[(2 * at + 1) * own : (2 * at + 2) * own, :]
        ref[total * SUB - halo :, :] = _halo(after_ref, at, False)
    _sweeps(c_ref, f_ref, g, gz, w, u1, u2, None, HALO, total - HALO, True)
    rows = layers * SUB
    edge = EDGE * SUB
    settled_ref[edge : rows - edge, :] = u2_in[edge : rows - edge, :]
    settled_ref[:edge, :] = u2[halo : halo + edge, :]
    settled_ref[rows - edge :, :] = u2[span * SUB + halo : span * SUB + halo + edge, :]
    load.wait()

    owners = [owner_ref[0, k] for k in range(boxes)]
    sends = []
    for k in range(boxes):
        first, second = jnp.int32(k), jnp.int32(-1)
        for j in range(boxes):
            if j < k:
                first = jnp.where((owners[j] == owners[k]) & (first == k), j, first)
            if j > k:
                second = jnp.where(owners[j] == owners[k], j, second)

        @pl.when(first == k)
        def _():
            mixed_ref[pl.ds(0, box_rows, stride=2), :] = settled_ref[k * box_rows : (k + 1) * box_rows, :]
            start = pl.multiple_of(jnp.maximum(second, 0) * box_rows, box_rows)
            cells = settled_ref[pl.ds(start, box_rows), :]
            mixed_ref[pl.ds(1, box_rows, stride=2), :] = jnp.where(second >= 0, cells, 0.0)
            staged_ref[k] = mixed_ref[...].astype(BF16)

        sends.append(pltpu.make_async_copy(staged_ref.at[first], slots_ref.at[owners[k]], sems.at[k]))
        sends[-1].start()
    for send in sends:
        send.wait()


def coarse_kernel(layers, before_ref, after_ref, f_in, c_in, coarse_ref, c_ref, f_ref, *work):
    *g, gz, w, u1, t, u2, pair = work
    halo, rows = HALO * SUB, layers * SUB
    for at, (cells, ref) in enumerate(((f_in, f_ref), (c_in, c_ref))):
        _transposed(cells, ref, lambda row: row, layers, HALO)
        ref[:halo, :] = _halo(before_ref, at, True)
        ref[halo + rows :, :] = _halo(after_ref, at, False)
    _sweeps(c_ref, f_ref, g, gz, w, u1, u2, t, HALO, HALO + layers, True)
    _residual(u2, t, g, gz, pair, HALO, HALO + layers, 0)
    rows = coarse_ref.shape[0] - 16
    means = _pooled(pair, rows)
    peak = jnp.full((16, LANES), jnp.max(jnp.abs(means)), F32)
    power = jnp.floor(jnp.log2(jnp.clip(peak, 1e-30, 1e30)))
    coarse_ref[:rows, :] = means * jnp.exp2(-power)[:1, :]
    coarse_ref[rows:, :] = power


def spread_kernel(sizes, block_rows, box_rows, boxes, in_ref, out_ref):
    step = pl.program_id(0)
    x_count, y_count, core_count = sizes
    parts = []
    for d in range(8):
        device = step * 8 + d
        core, y, x = device % core_count, device // core_count % y_count, device // core_count // y_count
        start = ((y * core_count + core) * x_count + x) * block_rows
        power = in_ref[pl.ds(pl.multiple_of(start + boxes * box_rows, 16), 16), :]
        scale = jnp.exp2(power)[:1, :]
        for k in range(boxes):
            parts.append(in_ref[pl.ds(pl.multiple_of(start + k * box_rows, 16), box_rows), :] * scale)
    for at in range(0, len(parts), 8):
        tiles = jnp.swapaxes(jnp.stack(parts[at : at + 8]), 0, 1)
        for lane in range(box_rows):
            out_ref[at : at + 8, lane * LANES : (lane + 1) * LANES] = tiles[lane]


def _params(limit=VMEM_LIMIT):
    return pltpu.CompilerParams(vmem_limit_bytes=limit)


def _whole(count):
    return [pl.BlockSpec(memory_space=pltpu.VMEM)] * count


def _scratch(layers, count):
    return [pltpu.VMEM((layers * SUB, LANES), F32)] * count


def shards(sizes, source, conductivity, new_owner):
    layers, rows_y, rows_x = source.shape
    boxes = new_owner.shape[2]
    depth = layers // boxes
    group_count = lax.axis_size("grp")
    box_rows = depth * SUB
    coarse_rows = depth * SUB * LANES // 8 // LANES
    inner_boxes = boxes - 2
    f_in = jnp.transpose(source, (1, 2, 0)).reshape(rows_y * rows_x, layers)
    c_in = jnp.transpose(conductivity, (1, 2, 0)).reshape(rows_y * rows_x, layers)
    owners = new_owner.reshape(1, boxes)

    edge = jax.ShapeDtypeStruct((2 * SIDE * SUB, LANES), BF16)
    held = jax.ShapeDtypeStruct(f_in.shape, BF16)
    first, last, f_held, c_held = pl.pallas_call(
        functools.partial(edges_kernel, layers),
        out_shape=[edge, edge, held, held],
        in_specs=[pl.BlockSpec(memory_space=pltpu.HBM)] * 2,
        out_specs=_whole(4),
        scratch_shapes=_scratch(2 * SIDE, 2) + [pltpu.SemaphoreType.DMA((2,))],
        compiler_params=_params(),
        cost_estimate=pl.CostEstimate(flops=10**7, bytes_accessed=10**6, transcendentals=0),
        name="edge_layers",
    )(*(pltpu.with_memory_space_constraint(cells, pltpu.HBM) for cells in (f_in, c_in)))
    everyone = ("x", "y", "core", "grp")
    count = lax.axis_size(everyone)
    before = lax.ppermute(last, everyone, [(i, i + 1) for i in range(count - 1)])
    after = lax.ppermute(first, everyone, [(i + 1, i) for i in range(count - 1)])

    slots_shape = (group_count, 2 * box_rows, LANES)
    hbm = pl.BlockSpec(memory_space=pltpu.HBM)
    near, u2, slots = pl.pallas_call(
        functools.partial(inner_kernel, layers),
        out_shape=[
            jax.ShapeDtypeStruct((4 * (EDGE + HALO) * SUB, LANES), F32),
            jax.ShapeDtypeStruct((layers * SUB, LANES), F32),
            pltpu.HBM(slots_shape, BF16),
        ],
        in_specs=_whole(2),
        out_specs=_whole(2) + [hbm],
        scratch_shapes=_scratch(layers, 9)
        + [pltpu.VMEM(slots_shape[1:], BF16), pltpu.SemaphoreType.DMA((group_count,))],
        compiler_params=_params(),
        cost_estimate=pl.CostEstimate(flops=10**8, bytes_accessed=10**7, transcendentals=0),
        name="inner_layers",
    )(f_held, c_held)

    total = 2 * (EDGE + 2 * HALO)
    slots = pl.pallas_call(
        functools.partial(outer_kernel, layers, box_rows, boxes),
        out_shape=jax.ShapeDtypeStruct(slots_shape, BF16),
        in_specs=[hbm] + _whole(4) + [hbm],
        out_specs=hbm,
        scratch_shapes=_scratch(total, 10)
        + _scratch(layers, 1)
        + _scratch(2 * depth, 1)
        + [
            pltpu.VMEM((boxes,) + slots_shape[1:], BF16),
            pltpu.SMEM((1, boxes), jnp.int32),
            pltpu.SemaphoreType.DMA((1,)),
            pltpu.SemaphoreType.DMA((boxes,)),
        ],
        input_output_aliases={5: 0},
        compiler_params=_params(),
        name="outer_layers",
    )(
        pltpu.with_memory_space_constraint(owners, pltpu.HBM),
        before,
        after,
        near,
        u2,
        pltpu.with_memory_space_constraint(slots, pltpu.HBM),
    )

    coarse = pl.pallas_call(
        functools.partial(coarse_kernel, layers),
        out_shape=jax.ShapeDtypeStruct((boxes * coarse_rows + 16, LANES), F32),
        in_specs=_whole(4),
        out_specs=pl.BlockSpec(memory_space=pltpu.VMEM),
        scratch_shapes=_scratch(layers + 2 * HALO, 11) + _scratch(layers // 2, 1),
        compiler_params=_params(),
        cost_estimate=pl.CostEstimate(flops=10**8, bytes_accessed=10**7, transcendentals=0),
        name="coarse_rows",
    )(before, after, f_held, c_held)

    correction = lax.all_to_all(slots, "grp", split_axis=0, concat_axis=0, tiled=True)
    correction = correction.reshape(group_count, box_rows, 2, LANES).transpose(0, 2, 1, 3)
    gathered = coarse.astype(F16)
    for axes in ("x", ("y", "core")):
        gathered = lax.all_gather(gathered, axes, axis=0, tiled=True)

    devices = sizes[0] * sizes[1] * sizes[2]
    coarse_all = pl.pallas_call(
        functools.partial(spread_kernel, sizes, coarse.shape[0], coarse_rows, boxes),
        out_shape=jax.ShapeDtypeStruct((devices * boxes, coarse_rows * LANES), F32),
        grid=(devices // 8,),
        in_specs=_whole(1),
        out_specs=pl.BlockSpec((8 * boxes, coarse_rows * LANES), lambda i: (i, 0)),
        compiler_params=_params(),
        name="spread_coarse",
    )(gathered.astype(F32))
    return (
        correction.reshape(1, 1, group_count, 2, box_rows * LANES),
        coarse_all[None],
    )


def solution(mesh):
    sizes = (4, 8, 2) if mesh.shape["box"] == 64 else (1, 8, 2)
    fine = Mesh(mesh.devices.reshape(sizes + (mesh.shape["grp"],)), ("x", "y", "core", "grp"))
    box = ("x", "y", "core")
    return jax.shard_map(
        functools.partial(shards, sizes),
        mesh=fine,
        in_specs=(
            P(box + ("grp",), None, None),
            P(box + ("grp",), None, None),
            P(box, "grp", None, None),
        ),
        out_specs=(P(box, "grp", None, None, None), P("grp", None, None)),
        check_vma=False,
    )
```

```python
import functools

import jax
import jax.numpy as jnp
from jax import lax
from jax.experimental import pallas as pl
from jax.experimental.pallas import tpu as pltpu
from jax.sharding import Mesh, PartitionSpec as P

WEIGHT = 0.8
F32, BF16, F16 = jnp.float32, jnp.bfloat16, jnp.float16
HALO = 3
STEP = 40
EDGE = 2
SIDE = 4
SUB, LANES = 8, 128
VMEM_LIMIT = 40 * 1024 * 1024


def _iota(shape, dim):
    return lax.broadcasted_iota(jnp.int32, shape, dim)


def _chunks(lo, hi, step, body):
    whole = (hi - lo) // step
    if whole:

        @pl.loop(0, whole)
        def _(i):
            body(lo + i * step, step)

    if lo + whole * step < hi:
        body(lo + whole * step, hi - lo - whole * step)


def _load(ref, layer, count, shift=0):
    if isinstance(layer, int):
        rows = ref[layer * SUB + shift : (layer + count) * SUB + shift, :]
    elif shift:
        rows = ref[pl.ds(layer * SUB + shift, count * SUB), :]
    else:
        rows = ref[pl.ds(pl.multiple_of(layer * SUB, SUB), count * SUB), :]
    return rows.reshape(count, SUB, LANES)


def _store(ref, layer, value):
    count = value.shape[0]
    rows = value.reshape(count * SUB, LANES)
    if isinstance(layer, int):
        ref[layer * SUB : (layer + count) * SUB, :] = rows
    else:
        ref[pl.ds(pl.multiple_of(layer * SUB, SUB), count * SUB), :] = rows


def _beside(ref, layer, count):
    here = _load(ref, layer, count)
    lane = _iota((1, SUB, LANES), 2)
    below = jnp.where(lane < 32, _load(ref, layer, count, 1), here)
    above = jnp.where(lane >= 96, _load(ref, layer, count, -1), here)
    return (
        pltpu.roll(here, LANES - 1, 2),
        pltpu.roll(here, 1, 2),
        pltpu.roll(below, LANES - 32, 2),
        pltpu.roll(above, 32, 2),
    )


def _transposed(cells_ref, out_ref, layer_of, layers, at=0):
    total = cells_ref.shape[1]
    pick = (_iota((layers, total), 1) == layer_of(_iota((layers, total), 0))).astype(BF16)
    for j in range(SUB):
        part = lax.dot_general(
            pick,
            cells_ref[j * LANES : (j + 1) * LANES, :],
            (((1,), (1,)), ((), ())),
            preferred_element_type=F32,
        )
        out_ref[pl.ds(at * SUB + j, layers, stride=SUB), :] = part


def _sweeps(c_ref, f_ref, g_refs, gz_ref, w_ref, u1_ref, u2_ref, t_ref, lo, hi, ends):
    lo, hi = lo - 2, hi + 2
    sub, lane = _iota((1, SUB, LANES), 1), _iota((1, SUB, LANES), 2)
    x, y = lane & 31, sub * 4 + (lane >> 5)
    sides = (x == 31, x == 0, y == 31, y == 0)
    halves = [jnp.where(side, 0.0, 0.5) for side in sides]
    outer = sum(side.astype(F32) for side in sides)

    def faces(layer, count):
        c = _load(c_ref, layer, count)
        after, before = _load(c_ref, layer + 1, count), _load(c_ref, layer - 1, count)
        gz, gz_before = 0.5 * (c + after), 0.5 * (c + before)
        diagonal = c * outer
        if ends:
            diagonal = diagonal + jnp.where(after > 0, gz, c) + jnp.where(before > 0, gz_before, c)
            gz = jnp.where((c > 0) & (after > 0), gz, 0.0)
        else:
            diagonal = diagonal + (gz + gz_before)
        _store(gz_ref, layer, gz)
        for half, g_ref, other in zip(halves, g_refs, _beside(c_ref, layer, count)):
            g = half * (c + other)
            diagonal = diagonal + g
            _store(g_ref, layer, g)
        if ends:
            diagonal = jnp.where(c > 0, diagonal, 1.0)
        inverse = pl.reciprocal(diagonal, approx=True)
        inverse = inverse * (2.0 - diagonal * inverse)
        inverse = inverse * (2.0 - diagonal * inverse)
        weight = WEIGHT * inverse
        _store(w_ref, layer, weight)
        _store(u1_ref, layer, weight * _load(f_ref, layer, count))

    _chunks(lo, hi, STEP, faces)
    lo, hi = lo + 1, hi - 1

    def second(layer, count):
        pulled = _pull(u1_ref, g_refs, gz_ref, layer, count)
        f = _load(f_ref, layer, count)
        _store(u2_ref, layer, _load(w_ref, layer, count) * ((2.0 - WEIGHT) * f + pulled))
        if t_ref is not None:
            _store(t_ref, layer, (1.0 - WEIGHT) ** 2 * f - WEIGHT * pulled)

    _chunks(lo, hi, STEP, second)


def _pull(u_ref, g_refs, gz_ref, layer, count):
    total = _load(gz_ref, layer, count) * _load(u_ref, layer + 1, count)
    total = total + _load(gz_ref, layer - 1, count) * _load(u_ref, layer - 1, count)
    for g_ref, other in zip(g_refs, _beside(u_ref, layer, count)):
        total = total + _load(g_ref, layer, count) * other
    return total


def _residual(u2_ref, t_ref, g_refs, gz_ref, pair_ref, lo, hi, pair_at):
    def body(layer, count):
        left = _load(t_ref, layer, count) + _pull(u2_ref, g_refs, gz_ref, layer, count)
        pairs = left.reshape(count // 2, 2, SUB, LANES)
        _store(pair_ref, (layer - lo) // 2 + pair_at, pairs[:, 0] + pairs[:, 1])

    _chunks(lo, hi, STEP, body)


def _pooled(pair_ref, rows):
    lane, to = _iota((LANES, LANES), 0), _iota((LANES, LANES), 1)
    place = (lane // 64) * 16 + (lane % 32) // 2
    total = jnp.zeros((rows, LANES), F32)
    for k in range(4):
        part = pair_ref[pl.ds(k, rows, stride=4), :]
        pick = jnp.where(to == place + 32 * k, 0.125, 0.0).astype(BF16)
        high = part.astype(BF16)
        rest = part - high.astype(F32)
        low = rest.astype(BF16)
        lowest = (rest - low.astype(F32)).astype(BF16)
        for term in (high, low, lowest):
            total = total + jnp.dot(term, pick, preferred_element_type=F32)
    return total


def edges_kernel(layers, f_in, c_in, first_ref, last_ref, f_held, c_held, f_ref, c_ref, sems):
    def layer_of(row):
        return jnp.where(row < SIDE, row, row + layers - 2 * SIDE)

    copies = [
        pltpu.make_async_copy(cells, held, sems.at[at])
        for at, (cells, held) in enumerate(((f_in, f_held), (c_in, c_held)))
    ]
    for copy in copies:
        copy.start()
    rows = SIDE * SUB
    for at, (copy, held, ref) in enumerate(zip(copies, (f_held, c_held), (f_ref, c_ref))):
        copy.wait()
        _transposed(held, ref, layer_of, 2 * SIDE)
        first_ref[at * rows : (at + 1) * rows, :] = ref[:rows, :].astype(BF16)
        last_ref[at * rows : (at + 1) * rows, :] = ref[rows:, :].astype(BF16)


def _halo(side_ref, at, last):
    rows = SIDE * SUB
    cells = side_ref[at * rows : (at + 1) * rows, :].astype(F32)
    return cells[rows - HALO * SUB :] if last else cells[: HALO * SUB]


def inner_kernel(layers, f_in, c_in, near_ref, u2_ref, slots_ref, c_ref, f_ref, *work):
    *g, gz, w, u1, blank_ref, sems = work
    blank_ref[...] = jnp.zeros(blank_ref.shape, BF16)
    blanks = [pltpu.make_async_copy(blank_ref, slots_ref.at[i], sems.at[i]) for i in range(slots_ref.shape[0])]
    for copy in blanks:
        copy.start()
    for cells, ref in ((f_in, f_ref), (c_in, c_ref)):
        _transposed(cells, ref, lambda row: row, layers)
    rows = (EDGE + HALO) * SUB
    for at, ref in enumerate((f_ref, c_ref)):
        near_ref[2 * at * rows : (2 * at + 1) * rows, :] = ref[:rows, :]
        near_ref[(2 * at + 1) * rows : (2 * at + 2) * rows, :] = ref[layers * SUB - rows :, :]
    _sweeps(c_ref, f_ref, g, gz, w, u1, u2_ref, None, EDGE + 1, layers - EDGE - 1, False)
    u2_ref[: EDGE * SUB, :] = jnp.zeros((EDGE * SUB, LANES), F32)
    u2_ref[(layers - EDGE) * SUB : layers * SUB, :] = jnp.zeros((EDGE * SUB, LANES), F32)
    for copy in blanks:
        copy.wait()


def outer_kernel(layers, box_rows, boxes, owner_in, before_ref, after_ref, near_ref, u2_in, slots_in, slots_ref, c_ref, f_ref, *work):
    del slots_in
    *g, gz, w, u1, u2, mixed_ref, staged_ref, owner_ref, owner_sem, sems = work
    load = pltpu.make_async_copy(owner_in, owner_ref, owner_sem.at[0])
    load.start()
    span = EDGE + 2 * HALO
    total = 2 * span
    halo, own = HALO * SUB, (EDGE + HALO) * SUB
    for at, ref in enumerate((f_ref, c_ref)):
        ref[:halo, :] = _halo(before_ref, at, True)
        ref[halo : span * SUB, :] = near_ref[2 * at * own : (2 * at + 1) * own, :]
        ref[span * SUB : total * SUB - halo, :] = near_ref[(2 * at + 1) * own : (2 * at + 2) * own, :]
        ref[total * SUB - halo :, :] = _halo(after_ref, at, False)
    _sweeps(c_ref, f_ref, g, gz, w, u1, u2, None, HALO, total - HALO, True)
    edge = EDGE * SUB
    late = 2 * (box_rows - edge)
    head, tail = u2[halo : halo + edge, :], u2[span * SUB + halo : span * SUB + halo + edge, :]
    load.wait()

    owners = [owner_ref[0, k] for k in range(boxes)]
    sends = []
    for k in range(boxes):
        first, second = jnp.int32(k), jnp.int32(-1)
        for j in range(boxes):
            if j < k:
                first = jnp.where((owners[j] == owners[k]) & (first == k), j, first)
            if j > k:
                second = jnp.where(owners[j] == owners[k], j, second)

        @pl.when(first == k)
        def _():
            mixed_ref[pl.ds(0, box_rows, stride=2), :] = u2_in[k * box_rows : (k + 1) * box_rows, :]
            start = pl.multiple_of(jnp.maximum(second, 0) * box_rows, box_rows)
            mixed_ref[pl.ds(1, box_rows, stride=2), :] = jnp.where(second >= 0, u2_in[pl.ds(start, box_rows), :], 0.0)
            if k == 0:
                mixed_ref[pl.ds(0, edge, stride=2), :] = head
            if k == boxes - 1:
                mixed_ref[pl.ds(late, edge, stride=2), :] = tail

            @pl.when(second == boxes - 1)
            def _():
                mixed_ref[pl.ds(late + 1, edge, stride=2), :] = tail

            staged_ref[k] = mixed_ref[...].astype(BF16)

        sends.append(pltpu.make_async_copy(staged_ref.at[first], slots_ref.at[owners[k]], sems.at[k]))
        sends[-1].start()
    for send in sends:
        send.wait()


def coarse_kernel(layers, before_ref, after_ref, f_in, c_in, coarse_ref, c_ref, f_ref, *work):
    *g, gz, w, u1, t, u2, pair = work
    halo, rows = HALO * SUB, layers * SUB
    for at, (cells, ref) in enumerate(((f_in, f_ref), (c_in, c_ref))):
        _transposed(cells, ref, lambda row: row, layers, HALO)
        ref[:halo, :] = _halo(before_ref, at, True)
        ref[halo + rows :, :] = _halo(after_ref, at, False)
    _sweeps(c_ref, f_ref, g, gz, w, u1, u2, t, HALO, HALO + layers, True)
    _residual(u2, t, g, gz, pair, HALO, HALO + layers, 0)
    rows = coarse_ref.shape[0] - 16
    means = _pooled(pair, rows)
    peak = jnp.full((16, LANES), jnp.max(jnp.abs(means)), F32)
    power = jnp.floor(jnp.log2(jnp.clip(peak, 1e-30, 1e30)))
    coarse_ref[:rows, :] = means * jnp.exp2(-power)[:1, :]
    coarse_ref[rows:, :] = power


def spread_kernel(sizes, block_rows, box_rows, boxes, in_ref, out_ref):
    step = pl.program_id(0)
    x_count, y_count, core_count = sizes
    parts = []
    for d in range(8):
        device = step * 8 + d
        core, y, x = device % core_count, device // core_count % y_count, device // core_count // y_count
        start = ((y * core_count + core) * x_count + x) * block_rows
        power = in_ref[pl.ds(pl.multiple_of(start + boxes * box_rows, 16), 16), :]
        scale = jnp.exp2(power)[:1, :]
        for k in range(boxes):
            parts.append(in_ref[pl.ds(pl.multiple_of(start + k * box_rows, 16), box_rows), :] * scale)
    for at in range(0, len(parts), 8):
        tiles = jnp.swapaxes(jnp.stack(parts[at : at + 8]), 0, 1)
        for lane in range(box_rows):
            out_ref[at : at + 8, lane * LANES : (lane + 1) * LANES] = tiles[lane]


def _params(limit=VMEM_LIMIT):
    return pltpu.CompilerParams(vmem_limit_bytes=limit)


def _whole(count):
    return [pl.BlockSpec(memory_space=pltpu.VMEM)] * count


def _scratch(layers, count):
    return [pltpu.VMEM((layers * SUB, LANES), F32)] * count


def shards(sizes, source, conductivity, new_owner):
    layers, rows_y, rows_x = source.shape
    boxes = new_owner.shape[2]
    depth = layers // boxes
    group_count = lax.axis_size("grp")
    box_rows = depth * SUB
    coarse_rows = depth * SUB * LANES // 8 // LANES
    inner_boxes = boxes - 2
    f_in = jnp.transpose(source, (1, 2, 0)).reshape(rows_y * rows_x, layers)
    c_in = jnp.transpose(conductivity, (1, 2, 0)).reshape(rows_y * rows_x, layers)
    owners = new_owner.reshape(1, boxes)

    edge = jax.ShapeDtypeStruct((2 * SIDE * SUB, LANES), BF16)
    held = jax.ShapeDtypeStruct(f_in.shape, BF16)
    first, last, f_held, c_held = pl.pallas_call(
        functools.partial(edges_kernel, layers),
        out_shape=[edge, edge, held, held],
        in_specs=[pl.BlockSpec(memory_space=pltpu.HBM)] * 2,
        out_specs=_whole(4),
        scratch_shapes=_scratch(2 * SIDE, 2) + [pltpu.SemaphoreType.DMA((2,))],
        compiler_params=_params(),
        cost_estimate=pl.CostEstimate(flops=10**7, bytes_accessed=10**6, transcendentals=0),
        name="edge_layers",
    )(*(pltpu.with_memory_space_constraint(cells, pltpu.HBM) for cells in (f_in, c_in)))
    everyone = ("x", "y", "core", "grp")
    count = lax.axis_size(everyone)
    before = lax.ppermute(last, everyone, [(i, i + 1) for i in range(count - 1)])
    after = lax.ppermute(first, everyone, [(i + 1, i) for i in range(count - 1)])

    slots_shape = (group_count, 2 * box_rows, LANES)
    hbm = pl.BlockSpec(memory_space=pltpu.HBM)
    near, u2, slots = pl.pallas_call(
        functools.partial(inner_kernel, layers),
        out_shape=[
            jax.ShapeDtypeStruct((4 * (EDGE + HALO) * SUB, LANES), F32),
            jax.ShapeDtypeStruct((layers * SUB, LANES), F32),
            pltpu.HBM(slots_shape, BF16),
        ],
        in_specs=_whole(2),
        out_specs=_whole(2) + [hbm],
        scratch_shapes=_scratch(layers, 9)
        + [pltpu.VMEM(slots_shape[1:], BF16), pltpu.SemaphoreType.DMA((group_count,))],
        compiler_params=_params(),
        cost_estimate=pl.CostEstimate(flops=10**8, bytes_accessed=10**7, transcendentals=0),
        name="inner_layers",
    )(f_held, c_held)

    total = 2 * (EDGE + 2 * HALO)
    slots = pl.pallas_call(
        functools.partial(outer_kernel, layers, box_rows, boxes),
        out_shape=jax.ShapeDtypeStruct(slots_shape, BF16),
        in_specs=[hbm] + _whole(4) + [hbm],
        out_specs=hbm,
        scratch_shapes=_scratch(total, 10)
        + _scratch(2 * depth, 1)
        + [
            pltpu.VMEM((boxes,) + slots_shape[1:], BF16),
            pltpu.SMEM((1, boxes), jnp.int32),
            pltpu.SemaphoreType.DMA((1,)),
            pltpu.SemaphoreType.DMA((boxes,)),
        ],
        input_output_aliases={5: 0},
        compiler_params=_params(),
        name="outer_layers",
    )(
        pltpu.with_memory_space_constraint(owners, pltpu.HBM),
        before,
        after,
        near,
        u2,
        pltpu.with_memory_space_constraint(slots, pltpu.HBM),
    )

    coarse = pl.pallas_call(
        functools.partial(coarse_kernel, layers),
        out_shape=jax.ShapeDtypeStruct((boxes * coarse_rows + 16, LANES), F32),
        in_specs=_whole(4),
        out_specs=pl.BlockSpec(memory_space=pltpu.VMEM),
        scratch_shapes=_scratch(layers + 2 * HALO, 11) + _scratch(layers // 2, 1),
        compiler_params=_params(),
        cost_estimate=pl.CostEstimate(flops=10**8, bytes_accessed=10**7, transcendentals=0),
        name="coarse_rows",
    )(before, after, f_held, c_held)

    correction = lax.all_to_all(slots, "grp", split_axis=0, concat_axis=0, tiled=True)
    correction = correction.reshape(group_count, box_rows, 2, LANES).transpose(0, 2, 1, 3)
    gathered = coarse.astype(F16)
    for axes in ("x", ("y", "core")):
        gathered = lax.all_gather(gathered, axes, axis=0, tiled=True)

    devices = sizes[0] * sizes[1] * sizes[2]
    coarse_all = pl.pallas_call(
        functools.partial(spread_kernel, sizes, coarse.shape[0], coarse_rows, boxes),
        out_shape=jax.ShapeDtypeStruct((devices * boxes, coarse_rows * LANES), F32),
        grid=(devices // 8,),
        in_specs=_whole(1),
        out_specs=pl.BlockSpec((8 * boxes, coarse_rows * LANES), lambda i: (i, 0)),
        compiler_params=_params(),
        name="spread_coarse",
    )(gathered.astype(F32))
    return (
        correction.reshape(1, 1, group_count, 2, box_rows * LANES),
        coarse_all[None],
    )


def solution(mesh):
    sizes = (4, 8, 2) if mesh.shape["box"] == 64 else (1, 8, 2)
    fine = Mesh(mesh.devices.reshape(sizes + (mesh.shape["grp"],)), ("x", "y", "core", "grp"))
    box = ("x", "y", "core")
    return jax.shard_map(
        functools.partial(shards, sizes),
        mesh=fine,
        in_specs=(
            P(box + ("grp",), None, None),
            P(box + ("grp",), None, None),
            P(box, "grp", None, None),
        ),
        out_specs=(P(box, "grp", None, None, None), P("grp", None, None)),
        check_vma=False,
    )
```
